512 devices in a mesh: dp: 64 (over x, y, core), tensor: 8 (over z).
Axes of the slice: x: 4, y: 8, z: 8, core: 2. Of those that a mesh axis runs over, the one named last changes fastest.
Arguments:
- tokens: bfloat16 [8192, 16384], P('dp', 'tensor'), may hold values from -60 to 60
- cotangent: bfloat16 [8192, 16384], P('dp', 'tensor'), may hold values from -16 to 16
- prompt_len: int32 [64], P('dp'), may hold values from 1 to 64
- resp_len: int32 [64], P('dp'), may hold values from 1 to 64
- ranks: int32 [64], P('dp'), may hold values from 0 to 7, as said below
- factors: float32 [8, 2048, 128], P('tensor', 'dp'), may hold values from -6 to 6
- first_moment: float32 [8, 2048, 128], P('tensor', 'dp'), may hold values from -8.286408e-05 to 8.286408e-05
- second_moment: float32 [8, 2048, 128], P('tensor', 'dp'), may hold values from 4.7683715e-12 to 9.536744e-10
- base_weight: bfloat16 [16384, 16384], P('dp', 'tensor'), may hold values from -0.046875 to 0.046875
- gain: float32 [16384], P('tensor'), may hold values from 0.5 to 1.5
- state: bfloat16 [16, 16384], P(None, 'tensor'), may hold values from -6 to 6
Outputs:
- new_factors: float32 [8, 2048, 128], P('tensor', 'dp')
- decoded: bfloat16 [16, 16384], P(None, 'tensor')
The draws below stay inside these ranges and needn't reach their ends.
Inputs may be any that keep to these rules, and one draw needn't show every extreme that they name: `ranks`: each aligned group of 8 consecutive sequences holds every rank once.
All inputs are finite; a program needn't handle non-finite values.
Results may differ from the reference program's by a relative error of at most 0.0065.
Values may be sent and summed in bfloat16 or wider, within the bound.
No kernel may reach another device: no remote copies, remote signals or barrier semaphores. Data moves between devices by JAX's collectives and lax.ppermute only.
A program may use at most 64 MiB of HBM per device.

```python
import math
import jax
import jax.numpy as jnp
from jax import lax

MODEL_WIDTH = 16384
ADAPTER_RANK = 64
SEQLEN = 128
GROUP = 8
BATCH = 16
DECODE_STEPS = 4
SEQS = 64
TOKENS = 8192
N_TENSOR = 8


def draw_ranks(key, part):
    key = jax.random.fold_in(key, 7)
    keys = jax.random.split(key, SEQS // GROUP)
    perms = jax.vmap(lambda k: jax.random.permutation(k, GROUP))(keys)
    return perms.reshape(-1).astype(jnp.int32)


def column_rise(top):
    block = MODEL_WIDTH // N_TENSOR
    place = (jnp.arange(MODEL_WIDTH, dtype=jnp.int32) % block).astype(jnp.float32) / block
    return jnp.exp(math.log(top) * place)


def draw_tokens(key, part):
    key = jax.random.fold_in(key, 11)
    values = jnp.clip(jax.random.normal(key, (TOKENS, MODEL_WIDTH), jnp.float32), -5.5, 5.5)
    scaled = values * column_rise(10.0)[None, :]
    return scaled.astype(jnp.bfloat16)


def plant(drawn, own_key, low, top_value):
    longest = drawn.shape.index(max(drawn.shape))
    spots = []
    for shift in (0, 1):
        where = [jax.random.randint(jax.random.fold_in(own_key, axis), (), 0, length) for axis, length in enumerate(drawn.shape)]
        where[longest] = (where[longest] + shift) % drawn.shape[longest]
        spots.append(tuple(where))
    return drawn.at[spots[0]].set(low).at[spots[1]].set(top_value)


def spiked(values, stream_key, source, target, blocks, factor):
    def block_of(position):
        return (jnp.arange(values.shape[position]) // (values.shape[position] // blocks)).reshape((-1,) + (1,) * (values.ndim - 1 - position))

    near = jax.random.permutation(stream_key, blocks)[block_of(target)]
    second = (block_of(target) + blocks // 2) % blocks
    return jnp.where((block_of(source) == near) | (block_of(source) == second), factor * values, values)


def steps_of(key, shape, pieces, low, largest):
    def one(position, parts):
        draws = jax.random.uniform(jax.random.fold_in(jax.random.fold_in(key, 6), position), (parts,), jnp.float32, low / len(pieces), largest / len(pieces))
        return jnp.repeat(jnp.exp(draws), shape[position] // parts).reshape((-1,) + (1,) * (len(shape) - position - 1))

    level = one(*pieces[0])
    for cut in pieces[1:]:
        level = level * one(*cut)
    return level


def gaussian(stream_key, shape, spread, reach, shards=(), held_as=jnp.bfloat16):
    result = jax.random.normal(stream_key, shape, jnp.float32) * spread
    if len(shards) > 0:
        result = steps_of(stream_key, shape, shards, -0.22, 0.18) * result
    return jnp.clip(result, min=-reach, max=reach).astype(held_as)


def gaussian_with(own_key, extent, spread, limit, cuts, heavy, held_as=jnp.bfloat16):
    drawn = spread * jax.random.normal(own_key, extent, jnp.float32)
    if cuts:
        drawn = drawn * steps_of(own_key, extent, cuts, -0.22, 0.18)
    return jnp.clip(spiked(drawn, jax.random.fold_in(own_key, 3), *heavy), -limit, limit).astype(held_as)


def setup_inputs(seed: int = 0) -> dict:
    splits = jax.random.split(jax.random.key(seed), 12)
    tokens = draw_tokens(jax.random.fold_in(splits[11], 71), 0)
    cotangent = gaussian_with(splits[1], (TOKENS, MODEL_WIDTH), 1.0, 16.0, ((0, 64), (1, 8)), (0, 1, 64, 4.0))
    prompt_len = plant(jax.random.randint(splits[2], (SEQS,), 1, SEQLEN // 2 + 1), jax.random.fold_in(splits[2], 1), 1, (SEQLEN // 2 + 1) - 1).astype(jnp.int32)
    resp_len = plant(jax.random.randint(splits[3], (SEQS,), 1, SEQLEN // 2 + 1), jax.random.fold_in(splits[3], 1), 1, (SEQLEN // 2 + 1) - 1).astype(jnp.int32)
    ranks = draw_ranks(jax.random.fold_in(splits[11], 71), 0)
    factors = gaussian(splits[5], (N_TENSOR, MODEL_WIDTH // N_TENSOR, 2 * ADAPTER_RANK), 1.0, 6.0, ((0, 8), (1, 64)), jnp.float32)
    first_moment = gaussian(splits[6], (N_TENSOR, MODEL_WIDTH // N_TENSOR, 2 * ADAPTER_RANK), (0.02 / (2 * MODEL_WIDTH * ADAPTER_RANK) ** 0.5), 8.286407683044672e-05, ((0, 8), (1, 64)), jnp.float32)
    second_moment = jnp.clip(jnp.exp(math.log(9.536743617033494e-10) - 5.2983174 * jax.random.uniform(splits[7], (N_TENSOR, MODEL_WIDTH // N_TENSOR, 2 * ADAPTER_RANK), jnp.float32) ** steps_of(splits[7], (N_TENSOR, MODEL_WIDTH // N_TENSOR, 2 * ADAPTER_RANK), ((0, 8), (1, 64)), -0.2, 0.2)), 4.768371461572052e-12, 9.536743617033494e-10)
    base_weight = gaussian(splits[8], (MODEL_WIDTH, MODEL_WIDTH), MODEL_WIDTH ** -0.5, 0.046875, ((0, 64), (1, 8)))
    gain = jnp.clip(1.0 + 0.1 * jax.random.normal(splits[9], (MODEL_WIDTH,), jnp.float32), 0.5, 1.5)
    state = gaussian(splits[10], (BATCH, MODEL_WIDTH), 1.0, 6.0, ((1, 8),))
    return {"tokens": tokens, "cotangent": cotangent, "prompt_len": prompt_len, "resp_len": resp_len, "ranks": ranks, "factors": factors, "first_moment": first_moment, "second_moment": second_moment, "base_weight": base_weight, "gain": gain, "state": state}


adapter_alpha = 2.0
beta_one = 0.9
beta_two = 0.999
rate = 0.1
clip_norm = 1.0
adam_count = 200.0

def reference(tokens, cotangent, prompt_len, resp_len, ranks, factors, first_moment, second_moment, base_weight, gain, state):
    adapter_scale = adapter_alpha / (ADAPTER_RANK * math.sqrt(MODEL_WIDTH))
    flat = factors.reshape(MODEL_WIDTH, 2 * ADAPTER_RANK)
    positions = jnp.arange(SEQLEN, dtype=jnp.int32)
    lower = prompt_len[:, None]
    upper = lower + resp_len[:, None]
    inside = (positions[None, :] >= lower) & (positions[None, :] < upper)
    advantage = (2 * ranks - (GROUP - 1)).astype(jnp.float32) / (GROUP - 1)
    per_seq = advantage / resp_len.astype(jnp.float32)
    weight = jnp.where(inside, per_seq[:, None], jnp.float32(0.0)).reshape(-1)
    weighted = (cotangent.astype(jnp.float32) * weight[:, None]).astype(jnp.bfloat16)
    low = flat.astype(jnp.bfloat16)
    hidden = jnp.dot(tokens, low[:, :ADAPTER_RANK], preferred_element_type=jnp.float32).astype(jnp.bfloat16)
    projected = jnp.dot(weighted, low[:, ADAPTER_RANK:], preferred_element_type=jnp.float32).astype(jnp.bfloat16)
    dims = (((0,), (0,)), ((), ()))
    grad_down = lax.dot_general(tokens, projected, dims, preferred_element_type=jnp.float32)
    grad_up = lax.dot_general(weighted, hidden, dims, preferred_element_type=jnp.float32)
    grads = adapter_scale * jnp.concatenate([grad_down, grad_up], axis=1)
    total = jnp.sqrt(jnp.sum(grads * grads))
    clip = jnp.minimum(jnp.float32(1.0), clip_norm / (total + 1e-06))
    grads = clip * grads
    moment_one = beta_one * first_moment.reshape(MODEL_WIDTH, 2 * ADAPTER_RANK) + (1.0 - beta_one) * grads
    moment_two = beta_two * second_moment.reshape(MODEL_WIDTH, 2 * ADAPTER_RANK) + (1.0 - beta_two) * grads * grads
    step_size = moment_one / (1.0 - beta_one ** adam_count) / (jnp.sqrt(moment_two / (1.0 - beta_two ** adam_count)) + 1e-08)
    updated = flat - rate * step_size
    down_new = updated[:, :ADAPTER_RANK]
    fresh_up_weight = updated[:, ADAPTER_RANK:]
    current = state
    for step in range(DECODE_STEPS):
        base = jnp.dot(current, base_weight, preferred_element_type=jnp.float32)
        lowrank = jnp.dot(current.astype(jnp.float32), down_new, precision=lax.Precision.HIGHEST)
        output = base + adapter_scale * jnp.dot(lowrank, fresh_up_weight.T, precision=lax.Precision.HIGHEST)
        resid = current.astype(jnp.float32) + output
        meansq = lax.optimization_barrier(jnp.mean(resid * resid, axis=1))
        current = (resid * lax.rsqrt(meansq + 1e-05)[:, None] * gain[None, :]).astype(jnp.bfloat16)
    return (updated.reshape(N_TENSOR, MODEL_WIDTH // N_TENSOR, 2 * ADAPTER_RANK), current)
```

```python
import math

import jax
import jax.numpy as jnp
from jax import lax
from jax.sharding import Mesh
from jax.sharding import PartitionSpec as P

MODEL_WIDTH = 16384
SEQLEN = 128
GROUP = 8
RANK = 64
BATCH = 16
BLOCK = 2048
TILE = 256
OWN = 32

adapter_alpha = 2.0
beta_one = 0.9
beta_two = 0.999
rate = 0.1
adam_count = 200.0
scale = adapter_alpha / (RANK * math.sqrt(MODEL_WIDTH))

bf16 = jnp.bfloat16
f32 = jnp.float32
HIGHEST = lax.Precision.HIGHEST

AXES = ("x", "ya", "yb", "yc", "core", "z")
DP = ("x", "ya", "yb", "yc", "core")
MAJOR = ("x", "ya")
MINOR = ("yb", "yc", "core")


def swap(chunks, axes):
    return lax.all_to_all(chunks, axes, 0, 0, tiled=False)


def share(piece, axes, count):
    return swap(jnp.broadcast_to(piece[None], (count,) + piece.shape), axes)


def high_low(value):
    high = lax.reduce_precision(value, 8, 7)
    return high.astype(bf16), (value - high).astype(bf16)


def body(
    tokens,
    cotangent,
    prompt_len,
    resp_len,
    ranks,
    factors,
    first_moment,
    second_moment,
    base_weight,
    gain,
    state,
):
    major = lax.axis_index(MAJOR)
    minor = lax.axis_index(MINOR)
    z = lax.axis_index("z")
    dp = lax.axis_index(DP)
    at_home = (z == major).astype(f32)
    quarter = dp % 4

    crossed = lax.ppermute(
        base_weight, ("x", "ya", "z"), [(a * 8 + b, b * 8 + a) for a in range(8) for b in range(8)]
    )
    crossed = lax.all_gather(crossed, MINOR, axis=0, tiled=True)
    crossed = lax.dynamic_slice_in_dim(crossed, minor * TILE, TILE, 1)

    positions = jnp.arange(SEQLEN, dtype=jnp.int32)
    lower = prompt_len[:, None]
    upper = lower + resp_len[:, None]
    inside = (positions[None, :] >= lower) & (positions[None, :] < upper)
    advantage = (2 * ranks - (GROUP - 1)).astype(f32) / (GROUP - 1)
    per_seq = advantage / resp_len.astype(f32)
    weight = jnp.where(inside, per_seq[:, None], f32(0.0)).reshape(-1)
    weighted = (cotangent.astype(f32) * weight[:, None]).astype(bf16)

    low = share(factors[0].astype(bf16), DP, 64).reshape(BLOCK, 2 * RANK)
    hidden = jnp.dot(tokens, low[:, :RANK], preferred_element_type=f32)
    projected = jnp.dot(weighted, low[:, RANK:], preferred_element_type=f32)
    parts = share(jnp.concatenate([hidden, projected], axis=1).astype(bf16), "z", 8)
    both = jnp.sum(parts.astype(f32), axis=0).astype(bf16)
    dims = (((0,), (0,)), ((), ()))
    grad_down = lax.dot_general(tokens, both[:, RANK:], dims, preferred_element_type=f32)
    grad_up = lax.dot_general(weighted, both[:, :RANK], dims, preferred_element_type=f32)
    grads = jnp.concatenate([grad_down, grad_up], axis=1).astype(bf16)
    pieces = swap(grads.reshape(64, OWN, 2 * RANK), DP)
    grads = scale * jnp.sum(pieces.astype(f32), axis=0)

    squared = jnp.broadcast_to(jnp.sum(grads * grads), (1, 128))
    squared = jnp.sum(share(squared, ("x", "core"), 8), axis=0)
    squared = jnp.sum(share(squared, ("ya", "yb", "yc", "z"), 64), axis=0)
    clip = jnp.minimum(f32(1.0), f32(1.0) / (jnp.sqrt(squared) + 1e-06))
    grads = clip * grads
    moment_one = beta_one * first_moment[0] + (1.0 - beta_one) * grads
    moment_two = beta_two * second_moment[0] + (1.0 - beta_two) * grads * grads
    step_size = (
        moment_one
        / (1.0 - beta_one**adam_count)
        / (jnp.sqrt(moment_two / (1.0 - beta_two**adam_count)) + 1e-08)
    )
    updated = factors[0] - rate * step_size

    block = share(updated.astype(bf16), DP, 64).reshape(BLOCK, 2 * RANK)
    down_block = block[:, :RANK]
    up_block = block[:, RANK:].astype(f32)

    def crossed_product(current):
        tile = lax.dynamic_slice_in_dim(current, minor * TILE, TILE, 1).astype(f32)
        return jnp.dot(current, crossed, preferred_element_type=f32) + at_home * tile

    base = crossed_product(state)
    inner = jnp.dot(state, down_block, preferred_element_type=f32)
    gain_tile = lax.dynamic_slice_in_dim(gain, minor * TILE, TILE, 0)
    sent = jnp.concatenate(
        [lax.dynamic_slice_in_dim(block, minor * TILE, TILE, 0)]
        + [part.reshape(-1, 128) for value in (base, inner, gain_tile) for part in high_low(value)],
        axis=0,
    )
    got = share(sent, "z", 8)
    mine = lax.dynamic_index_in_dim(got, major, 0, keepdims=False)
    total = jnp.sum(got[:, TILE : TILE + 80].astype(f32), axis=0)
    base = (total[0:32] + total[32:64]).reshape(BATCH, TILE)
    inner = (total[64:72] + total[72:80]).reshape(BATCH, RANK)
    gain_tile = mine[TILE + 80 :].astype(f32)
    gain_tile = (gain_tile[0:2] + gain_tile[2:4]).reshape(TILE)
    down_tile = mine[:TILE, :RANK]
    up_tile = mine[:TILE, RANK:].astype(f32)
    resid = base + scale * jnp.dot(inner, up_tile.T, precision=HIGHEST)

    own_gain = lax.dynamic_slice_in_dim(gain.reshape(4, 4, 128), quarter, 1, 0)[0]

    def tile_to_own(resid):
        sums = jnp.sum(resid * resid, axis=1)
        current = (resid * gain_tile[None, :]).astype(bf16)
        part = jnp.dot(current, base_weight, preferred_element_type=f32)
        thin = jnp.dot(current, down_tile, preferred_element_type=f32)
        part = part + scale * jnp.dot(thin, up_block.T, precision=HIGHEST)
        home = lax.dynamic_update_slice(
            jnp.zeros((BATCH, BLOCK), f32), at_home * current.astype(f32), (0, minor * TILE)
        )
        part = (part + home).reshape(64, 4, 128)
        sums = jnp.broadcast_to(sums[:, None, None, None], (BATCH, 4, 4, 128)).reshape(64, 4, 128)
        got = jnp.sum(swap(jnp.concatenate([part, sums], axis=1), DP), axis=0)
        return got[:4] * lax.rsqrt(got[4:] / MODEL_WIDTH + 1e-05)

    own = tile_to_own(resid)
    current = share((own * own_gain).astype(bf16), DP, 64).reshape(BATCH, BLOCK)

    before = current.astype(f32) / gain[None, :]
    sums = jnp.sum(before * before, axis=1)
    inner = jnp.dot(current, down_block, preferred_element_type=f32)
    part = crossed_product(current) + scale * jnp.dot(inner, up_tile.T, precision=HIGHEST)
    sent = jnp.concatenate([part, jnp.broadcast_to(sums[:, None], (BATCH, 128))], axis=1)
    got = jnp.sum(share(sent, "z", 8), axis=0)
    resid = got[:, :TILE] * lax.rsqrt(got[:, TILE : TILE + 1] / MODEL_WIDTH + 1e-05)

    own = tile_to_own(resid)
    sums = jnp.broadcast_to(jnp.sum(own * own), (1, 128))
    sums = jnp.sum(share(sums, ("yc", "core", "z"), 32), axis=0)
    own = (own * lax.rsqrt(sums / MODEL_WIDTH + 1e-05) * own_gain).astype(bf16)
    result = share(own, DP, 64).reshape(BATCH, BLOCK)
    return (updated[None], result)


def solution(mesh):
    fine = Mesh(mesh.devices.reshape(4, 2, 2, 2, 2, 8), AXES)
    return jax.shard_map(
        body,
        mesh=fine,
        in_specs=(
            P(DP, "z"),
            P(DP, "z"),
            P(DP),
            P(DP),
            P(DP),
            P("z", DP, None),
            P("z", DP, None),
            P("z", DP, None),
            P(DP, "z"),
            P("z"),
            P(None, "z"),
        ),
        out_specs=(P("z", DP, None), P(None, "z")),
        check_vma=False,
    )
```

```python
import math

import jax
import jax.numpy as jnp
from jax import lax
from jax.sharding import Mesh
from jax.sharding import PartitionSpec as P

MODEL_WIDTH = 16384
SEQLEN = 128
GROUP = 8
DECODE_STEPS = 4
RANK = 64
BATCH = 16
BLOCK = 2048
TILE = 256
OWN = 32

adapter_alpha = 2.0
beta_one = 0.9
beta_two = 0.999
rate = 0.1
adam_count = 200.0
scale = adapter_alpha / (RANK * math.sqrt(MODEL_WIDTH))

bf16 = jnp.bfloat16
f32 = jnp.float32
HIGHEST = lax.Precision.HIGHEST

AXES = ("x", "ya", "yb", "yc", "core", "z")
DP = ("x", "ya", "yb", "yc", "core")
MAJOR = ("x", "ya")
MINOR = ("yb", "yc", "core")
CROSS = ("x", "ya", "z")


def swap(chunks, axes):
    return lax.all_to_all(chunks, axes, 0, 0, tiled=False)


def share(piece, axes, count):
    return swap(jnp.broadcast_to(piece[None], (count,) + piece.shape), axes)


def high_low(value):
    high = lax.reduce_precision(value, 8, 7)
    return high.astype(bf16), (value - high).astype(bf16)


def chunks_of(value):
    return value.reshape(8, 2, 8, TILE).transpose(0, 2, 1, 3).reshape(64, 4, 128)


def body(
    tokens,
    cotangent,
    prompt_len,
    resp_len,
    ranks,
    factors,
    first_moment,
    second_moment,
    base_weight,
    gain,
    state,
):
    major = lax.axis_index(MAJOR)
    minor = lax.axis_index(MINOR)
    z = lax.axis_index("z")

    swapped = [(a * 8 + b, b * 8 + a) for a in range(8) for b in range(8)]
    old = lax.ppermute(
        jnp.concatenate([factors[0], first_moment[0], second_moment[0]], axis=0), DP, swapped
    )

    positions = jnp.arange(SEQLEN, dtype=jnp.int32)
    lower = prompt_len[:, None]
    upper = lower + resp_len[:, None]
    inside = (positions[None, :] >= lower) & (positions[None, :] < upper)
    advantage = (2 * ranks - (GROUP - 1)).astype(f32) / (GROUP - 1)
    per_seq = advantage / resp_len.astype(f32)
    weight = jnp.where(inside, per_seq[:, None], f32(0.0)).reshape(-1)
    weighted = (cotangent.astype(f32) * weight[:, None]).astype(bf16)

    low = share(factors[0].astype(bf16), DP, 64).reshape(BLOCK, 2 * RANK)
    hidden = jnp.dot(tokens, low[:, :RANK], preferred_element_type=f32)
    projected = jnp.dot(weighted, low[:, RANK:], preferred_element_type=f32)
    state_tile = lax.dynamic_slice_in_dim(state, minor * TILE, TILE, 1)
    sent = jnp.concatenate(
        [jnp.concatenate([hidden, projected], axis=1).astype(bf16), state_tile.reshape(32, 128)],
        axis=0,
    )
    got = share(sent, "z", 8)
    both = jnp.sum(got[:, :SEQLEN].astype(f32), axis=0).astype(bf16)
    states = got[:, SEQLEN:].reshape(8, BATCH, TILE)

    dims = (((0,), (0,)), ((), ()))
    grad_down = lax.dot_general(tokens, both[:, RANK:], dims, preferred_element_type=f32)
    grad_up = lax.dot_general(weighted, both[:, :RANK], dims, preferred_element_type=f32)
    grads = jnp.concatenate([grad_down, grad_up], axis=1).astype(bf16)
    grads = grads.reshape(8, 8, OWN, 2 * RANK).transpose(1, 0, 2, 3).reshape(64, OWN, 2 * RANK)
    first = lax.dynamic_index_in_dim(states, major, 0, keepdims=False)
    first = chunks_of(jnp.dot(first, base_weight, preferred_element_type=f32))
    pieces = swap(jnp.concatenate([grads, *high_low(first)], axis=1), DP).astype(f32)
    pieces = jnp.sum(pieces, axis=0)
    grads = scale * pieces[:OWN]
    own_state = lax.dynamic_slice(state, (2 * major, minor * TILE), (2, TILE)).astype(f32)
    own_base = (pieces[OWN : OWN + 4] + pieces[OWN + 4 :]).reshape(2, TILE) + own_state

    squared = jnp.broadcast_to(jnp.sum(grads * grads), (1, 128))
    squared = jnp.sum(share(squared, ("x", "core"), 8), axis=0)
    squared = jnp.sum(share(squared, ("ya", "yb", "yc", "z"), 64), axis=0)
    clip = jnp.minimum(f32(1.0), f32(1.0) / (jnp.sqrt(squared) + 1e-06))
    grads = clip * grads
    moment_one = beta_one * old[OWN : 2 * OWN] + (1.0 - beta_one) * grads
    moment_two = beta_two * old[2 * OWN :] + (1.0 - beta_two) * grads * grads
    step_size = (
        moment_one
        / (1.0 - beta_one**adam_count)
        / (jnp.sqrt(moment_two / (1.0 - beta_two**adam_count)) + 1e-08)
    )
    updated = old[:OWN] - rate * step_size
    new_factors = lax.ppermute(updated, DP, swapped)[None]

    own_gain = lax.dynamic_slice_in_dim(gain, minor * TILE, TILE, 0)
    sent = jnp.concatenate(
        [
            updated.astype(bf16),
            *[part.reshape(-1, 128) for value in (own_base, own_gain) for part in high_low(value)],
        ],
        axis=0,
    )
    got = share(sent, CROSS, 64).reshape(8, 8, OWN + 12, 128)
    home = lax.dynamic_index_in_dim(got, major, 1, keepdims=False)
    near = lax.dynamic_index_in_dim(got[:, :, :OWN, RANK:], z, 1, keepdims=False)
    down_tile = home[:, :OWN, :RANK].reshape(TILE, RANK)
    up_tile = home[:, :OWN, RANK:].reshape(TILE, RANK).astype(f32)
    up_near = near.reshape(TILE, RANK).astype(f32)
    rest = home[:, OWN:].astype(f32)
    base = (rest[:, 0:4] + rest[:, 4:8]).reshape(BATCH, TILE)
    tile_gain = (rest[0, 8:10] + rest[0, 10:12]).reshape(TILE)

    states = states.reshape(8, BATCH, 8, OWN).transpose(1, 2, 0, 3).reshape(BATCH, BLOCK)
    down_all = got[:, :, :OWN, :RANK].reshape(BLOCK, RANK)
    inner = jnp.dot(states, down_all, preferred_element_type=f32)
    inner = jnp.sum(share(inner.reshape(8, 128), MINOR, 8), axis=0).reshape(BATCH, RANK)
    resid = base + scale * jnp.dot(inner, up_tile.T, precision=HIGHEST)
    inner = lax.dynamic_slice_in_dim(inner, 2 * major, 2, 0)
    own = own_base + scale * jnp.dot(inner, up_near.T, precision=HIGHEST)
    own = (own * own_gain).astype(bf16)
    current = (resid * tile_gain).astype(bf16)

    for step in range(1, DECODE_STEPS):
        if step > 1:
            current = share(own.reshape(4, 128), CROSS, 64).reshape(8, 8, 4, 128)
            current = lax.dynamic_index_in_dim(current, major, 1, keepdims=False)
            current = current.reshape(BATCH, TILE)
            resid = current.astype(f32) / tile_gain
        sums = jnp.sum(resid * resid, axis=1)
        part = jnp.dot(current, base_weight, preferred_element_type=f32)
        thin = jnp.dot(current, down_tile, preferred_element_type=f32)
        pairs = jnp.stack(
            [thin.reshape(8, 128), jnp.broadcast_to(sums[:, None], (BATCH, 64)).reshape(8, 128)],
            axis=1,
        )
        pairs = jnp.broadcast_to(pairs[:, None], (8, 8, 2, 128)).reshape(64, 2, 128)
        got = jnp.sum(swap(jnp.concatenate([chunks_of(part), pairs], axis=1), DP), axis=0)
        thin = got[4].reshape(2, RANK)
        norm = lax.rsqrt(got[5].reshape(2, 64)[:, :1] / MODEL_WIDTH + 1e-05)
        total = own.astype(f32) + got[:4].reshape(2, TILE)
        resid = norm * (total + scale * jnp.dot(thin, up_near.T, precision=HIGHEST))
        own = (resid * own_gain).astype(bf16)

    sums = jnp.broadcast_to(jnp.sum(resid * resid, axis=1)[:, None], (2, 64)).reshape(1, 128)
    sums = jnp.sum(share(sums, ("yb", "yc", "core", "z"), 64), axis=0).reshape(2, 64)[:, :1]
    own = (resid * lax.rsqrt(sums / MODEL_WIDTH + 1e-05) * own_gain).astype(bf16)
    result = share(own.reshape(4, 128), DP, 64)
    result = result.reshape(8, 8, 2, TILE).transpose(0, 2, 1, 3).reshape(BATCH, BLOCK)
    return (new_factors, result)


def solution(mesh):
    fine = Mesh(mesh.devices.reshape(4, 2, 2, 2, 2, 8), AXES)
    return jax.shard_map(
        body,
        mesh=fine,
        in_specs=(
            P(DP, "z"),
            P(DP, "z"),
            P(DP),
            P(DP),
            P(DP),
            P("z", DP, None),
            P("z", DP, None),
            P("z", DP, None),
            P(DP, "z"),
            P("z"),
            P(None, "z"),
        ),
        out_specs=(P("z", DP, None), P(None, "z")),
        check_vma=False,
    )
```

```python
import math

import jax
import jax.numpy as jnp
from jax import lax
from jax.sharding import Mesh
from jax.sharding import PartitionSpec as P

MODEL_WIDTH = 16384
SEQLEN = 128
GROUP = 8
DECODE_STEPS = 4
RANK = 64
BATCH = 16
BLOCK = 2048
TILE = 256
OWN = 32

adapter_alpha = 2.0
beta_one = 0.9
beta_two = 0.999
rate = 0.1
adam_count = 200.0
scale = adapter_alpha / (RANK * math.sqrt(MODEL_WIDTH))

bf16 = jnp.bfloat16
f32 = jnp.float32
HIGHEST = lax.Precision.HIGHEST

AXES = ("x", "ya", "yb", "yc", "core", "z")
DP = ("x", "ya", "yb", "yc", "core")
Y = ("ya", "yb", "yc")
XY = ("x", "ya", "yb", "yc")


def swap(chunks, axes):
    return lax.all_to_all(chunks, axes, 0, 0, tiled=False)


def share(piece, axes, count):
    return swap(jnp.broadcast_to(piece[None], (count,) + piece.shape), axes)


def core_swap(value):
    return lax.ppermute(value, "core", [(0, 1), (1, 0)])


def high_low(value):
    high = lax.reduce_precision(value, 8, 7)
    return high.astype(bf16), (value - high).astype(bf16)


def pick(value, index, axis):
    return lax.dynamic_index_in_dim(value, index, axis, keepdims=False)


def body(
    tokens,
    cotangent,
    prompt_len,
    resp_len,
    ranks,
    factors,
    first_moment,
    second_moment,
    base_weight,
    gain,
    state,
):
    x = lax.axis_index("x")
    y = lax.axis_index(Y)
    core = lax.axis_index("core")
    z = lax.axis_index("z")
    major = lax.axis_index(("x", "ya"))
    minor = lax.axis_index(("yb", "yc", "core"))
    part = x * 2 + core

    rows = lax.all_gather(base_weight, Y, axis=0, tiled=True)

    there = [(c * 8 + r, r * 2 + c) for r in range(8) for c in range(2)]
    back = [(b, a) for a, b in there]
    old = lax.ppermute(
        jnp.concatenate([factors[0], first_moment[0], second_moment[0]], axis=0), Y + ("core",), there
    )

    positions = jnp.arange(SEQLEN, dtype=jnp.int32)
    lower = prompt_len[:, None]
    upper = lower + resp_len[:, None]
    inside = (positions[None, :] >= lower) & (positions[None, :] < upper)
    advantage = (2 * ranks - (GROUP - 1)).astype(f32) / (GROUP - 1)
    per_seq = advantage / resp_len.astype(f32)
    weight = jnp.where(inside, per_seq[:, None], f32(0.0)).reshape(-1)
    weighted = (cotangent.astype(f32) * weight[:, None]).astype(bf16)

    mine = share(factors[0].astype(bf16), XY, 32)
    other = core_swap(mine)
    low = jnp.where(core == 0, jnp.stack([mine, other], 1), jnp.stack([other, mine], 1))
    low = low.reshape(BLOCK, 2 * RANK)
    hidden = jnp.dot(tokens, low[:, :RANK], preferred_element_type=f32)
    projected = jnp.dot(weighted, low[:, RANK:], preferred_element_type=f32)
    state_tile = lax.dynamic_slice_in_dim(state, minor * TILE, TILE, 1)
    sent = jnp.concatenate(
        [jnp.concatenate([hidden, projected], axis=1).astype(bf16), state_tile.reshape(32, 128)],
        axis=0,
    )
    got = share(sent, "z", 8)
    both = jnp.sum(got[:, :SEQLEN].astype(f32), axis=0).astype(bf16)
    first = pick(got[:, SEQLEN:], major, 0).reshape(BATCH, TILE)

    dims = (((0,), (0,)), ((), ()))
    grad_down = lax.dot_general(tokens, both[:, RANK:], dims, preferred_element_type=f32)
    grad_up = lax.dot_general(weighted, both[:, :RANK], dims, preferred_element_type=f32)
    grads = jnp.concatenate([grad_down, grad_up], axis=1).astype(bf16).reshape(4, 2, 8, OWN, 128)
    first = jnp.dot(first, base_weight, preferred_element_type=f32)
    first = first.reshape(8, 2, 4, 2, TILE)

    def half(which):
        base = pick(first, which, 3).transpose(2, 0, 1, 3).reshape(32, 4, 128)
        return pick(grads, which, 1).reshape(32, OWN, 128), base

    give, give_base = half(1 - core)
    keep, keep_base = half(core)
    got = core_swap(jnp.concatenate([give, *high_low(give_base)], axis=1)).astype(f32)
    keep = (keep.astype(f32) + got[:, :OWN]).astype(bf16)
    keep_base = keep_base + got[:, OWN : OWN + 4] + got[:, OWN + 4 :]
    pieces = swap(jnp.concatenate([keep, *high_low(keep_base)], axis=1), XY).astype(f32)
    pieces = jnp.sum(pieces, axis=0)
    grads = scale * pieces[:OWN]
    own_state = lax.dynamic_slice(state, (2 * y, part * TILE), (2, TILE))
    own_base = (pieces[OWN : OWN + 4] + pieces[OWN + 4 :]).reshape(2, TILE)
    own_base = own_base + own_state.astype(f32)

    squared = jnp.broadcast_to(jnp.sum(grads * grads), (1, 128))
    squared = jnp.sum(share(squared, ("yb", "yc", "core", "z"), 64), axis=0)
    squared = jnp.sum(share(squared, ("x", "ya"), 8), axis=0)
    clip = jnp.minimum(f32(1.0), f32(1.0) / (jnp.sqrt(squared) + 1e-06))
    grads = clip * grads
    moment_one = beta_one * old[OWN : 2 * OWN] + (1.0 - beta_one) * grads
    moment_two = beta_two * old[2 * OWN :] + (1.0 - beta_two) * grads * grads
    step_size = (
        moment_one
        / (1.0 - beta_one**adam_count)
        / (jnp.sqrt(moment_two / (1.0 - beta_two**adam_count)) + 1e-08)
    )
    updated = old[:OWN] - rate * step_size
    new_factors = lax.ppermute(updated, Y + ("core",), back)[None]

    near = share(updated.astype(bf16), Y, 8).reshape(TILE, 2 * RANK)
    down = near[:, :RANK]
    up = near[:, RANK:].astype(f32).T
    own_gain = lax.dynamic_slice_in_dim(gain, part * TILE, TILE, 0)

    def spread(pair):
        return jnp.broadcast_to(pair[:, None], (2, 64)).reshape(1, 128)

    thin = jnp.dot(own_state, down, preferred_element_type=f32).reshape(1, 128)
    thin = jnp.sum(share(thin, ("x", "core", "z"), 64), axis=0).reshape(2, RANK)
    resid = own_base + scale * jnp.dot(thin, up, precision=HIGHEST)

    for step in range(1, DECODE_STEPS):
        own = (resid * own_gain).astype(bf16)
        thin = jnp.dot(own, down, preferred_element_type=f32).reshape(1, 128)
        pairs = jnp.concatenate([thin, spread(jnp.sum(resid * resid, axis=1))], axis=0)
        sent = jnp.concatenate([own.reshape(4, 128), *high_low(pairs)], axis=0)
        got = share(sent, ("x", "z"), 32).reshape(4, 8, 8, 128)
        current = pick(got[:, :, :4].reshape(4, 4, 2, 2, TILE), x, 1)
        current = current.transpose(2, 1, 0, 3).reshape(2, BLOCK)
        pairs = jnp.sum(got[:, :, 4:].astype(f32), axis=(0, 1))
        pairs = 0.25 * (pairs[:2] + pairs[2:])
        sums = jnp.dot(current, rows, preferred_element_type=f32)
        sums = sums.reshape(2, 8, TILE).transpose(1, 0, 2).reshape(8, 4, 128)
        sent = jnp.concatenate([sums, jnp.broadcast_to(pairs[None], (8, 2, 128))], axis=1)
        got = jnp.sum(swap(sent, ("x", "core")), axis=0)
        thin = got[4].reshape(2, RANK)
        norm = lax.rsqrt(got[5].reshape(2, 64)[:, :1] / MODEL_WIDTH + 1e-05)
        total = own.astype(f32) + got[:4].reshape(2, TILE)
        resid = norm * (total + scale * jnp.dot(thin, up, precision=HIGHEST))

    sums = jnp.sum(share(spread(jnp.sum(resid * resid, axis=1)), ("x", "core", "z"), 64), axis=0)
    norm = lax.rsqrt(sums.reshape(2, 64)[:, :1] / MODEL_WIDTH + 1e-05)
    own = (resid * norm * own_gain).astype(bf16)
    result = share(own.reshape(4, 128), DP, 64).reshape(4, 8, 2, 2, TILE)
    result = result.transpose(1, 3, 0, 2, 4).reshape(BATCH, BLOCK)
    return (new_factors, result)


def solution(mesh):
    fine = Mesh(mesh.devices.reshape(4, 2, 2, 2, 2, 8), AXES)
    return jax.shard_map(
        body,
        mesh=fine,
        in_specs=(
            P(DP, "z"),
            P(DP, "z"),
            P(DP),
            P(DP),
            P(DP),
            P("z", DP, None),
            P("z", DP, None),
            P("z", DP, None),
            P(DP, "z"),
            P("z"),
            P(None, "z"),
        ),
        out_specs=(P("z", DP, None), P(None, "z")),
        check_vma=False,
    )
```

```python
import math

import jax
import jax.numpy as jnp
from jax import lax
from jax.sharding import Mesh
from jax.sharding import PartitionSpec as P

MODEL_WIDTH = 16384
SEQLEN = 128
GROUP = 8
DECODE_STEPS = 4
RANK = 64
BATCH = 16
BLOCK = 2048
TILE = 256
OWN = 32

adapter_alpha = 2.0
beta_one = 0.9
beta_two = 0.999
rate = 0.1
adam_count = 200.0
scale = adapter_alpha / (RANK * math.sqrt(MODEL_WIDTH))

bf16 = jnp.bfloat16
f32 = jnp.float32
HIGHEST = lax.Precision.HIGHEST

AXES = ("x", "ya", "yb", "yc", "core", "z")
DP = ("x", "ya", "yb", "yc", "core")
Y = ("ya", "yb", "yc")
XY = ("x", "ya", "yb", "yc")


def swap(chunks, axes):
    return lax.all_to_all(chunks, axes, 0, 0, tiled=False)


def share(piece, axes, count):
    return swap(jnp.broadcast_to(piece[None], (count,) + piece.shape), axes)


def core_swap(value):
    return lax.ppermute(value, "core", [(0, 1), (1, 0)])


def high_low(value):
    high = lax.reduce_precision(value, 8, 7)
    return high.astype(bf16), (value - high).astype(bf16)


def pick(value, index, axis):
    return lax.dynamic_index_in_dim(value, index, axis, keepdims=False)


def body(
    tokens,
    cotangent,
    prompt_len,
    resp_len,
    ranks,
    factors,
    first_moment,
    second_moment,
    base_weight,
    gain,
    state,
):
    x = lax.axis_index("x")
    y = lax.axis_index(Y)
    core = lax.axis_index("core")
    z = lax.axis_index("z")
    major = lax.axis_index(("x", "ya"))
    minor = lax.axis_index(("yb", "yc", "core"))
    part = x * 2 + core

    there = [(c * 8 + r, r * 2 + c) for r in range(8) for c in range(2)]
    back = [(b, a) for a, b in there]
    old = lax.ppermute(
        jnp.concatenate([factors[0], first_moment[0], second_moment[0]], axis=0), Y + ("core",), there
    )

    positions = jnp.arange(SEQLEN, dtype=jnp.int32)
    lower = prompt_len[:, None]
    upper = lower + resp_len[:, None]
    inside = (positions[None, :] >= lower) & (positions[None, :] < upper)
    advantage = (2 * ranks - (GROUP - 1)).astype(f32) / (GROUP - 1)
    per_seq = advantage / resp_len.astype(f32)
    weight = jnp.where(inside, per_seq[:, None], f32(0.0)).reshape(-1)
    weighted = (cotangent.astype(f32) * weight[:, None]).astype(bf16)

    mine = share(factors[0].astype(bf16), XY, 32)
    mine, rows = lax.optimization_barrier((mine, base_weight))
    rows = lax.all_gather(rows, Y, axis=0, tiled=True)
    other = core_swap(mine)
    low = jnp.where(core == 0, jnp.stack([mine, other], 1), jnp.stack([other, mine], 1))
    low = low.reshape(BLOCK, 2 * RANK)
    hidden = jnp.dot(tokens, low[:, :RANK], preferred_element_type=f32)
    projected = jnp.dot(weighted, low[:, RANK:], preferred_element_type=f32)
    state_tile = lax.dynamic_slice_in_dim(state, minor * TILE, TILE, 1)
    sent = jnp.concatenate(
        [jnp.concatenate([hidden, projected], axis=1).astype(bf16), state_tile.reshape(32, 128)],
        axis=0,
    )
    got = share(sent, "z", 8)
    both = jnp.sum(got[:, :SEQLEN].astype(f32), axis=0).astype(bf16)
    first = pick(got[:, SEQLEN:], major, 0).reshape(BATCH, TILE)

    dims = (((0,), (0,)), ((), ()))
    grad_down = lax.dot_general(tokens, both[:, RANK:], dims, preferred_element_type=f32)
    grad_up = lax.dot_general(weighted, both[:, :RANK], dims, preferred_element_type=f32)
    grads = jnp.concatenate([grad_down, grad_up], axis=1).astype(bf16).reshape(4, 2, TILE, 128)
    first = jnp.dot(first, base_weight, preferred_element_type=f32)
    first = first.reshape(8, 2, 4, 2, TILE)

    def half(which):
        base = pick(first, which, 3).transpose(2, 0, 1, 3).reshape(4, 32, 128)
        return pick(grads, which, 1), base

    give, give_base = half(1 - core)
    keep, keep_base = half(core)
    got = core_swap(jnp.concatenate([give, *high_low(give_base)], axis=1)).astype(f32)
    keep = (keep.astype(f32) + got[:, :TILE]).astype(bf16)
    keep_base = keep_base + got[:, TILE : TILE + 32] + got[:, TILE + 32 :]
    got = swap(jnp.concatenate([keep, *high_low(keep_base)], axis=1), "x").astype(f32)
    got = jnp.sum(got, axis=0)
    keep = got[:TILE].astype(bf16)
    keep_base = (got[TILE : TILE + 32] + got[TILE + 32 :]).reshape(8, 4, 128)
    keep = jnp.concatenate([keep, old[OWN:].astype(bf16)], axis=0)
    keep = jnp.broadcast_to(keep[None], (8, TILE + 2 * OWN, 128))
    got = swap(jnp.concatenate([keep, *high_low(keep_base)], axis=1), Y)
    grads = scale * jnp.sum(got[:, :TILE].astype(f32), axis=0)
    moments = got[:, TILE : TILE + 2 * OWN].astype(f32)
    own_base = jnp.sum(got[:, TILE + 2 * OWN :].astype(f32), axis=0)
    own_state = lax.dynamic_slice(state, (2 * y, part * TILE), (2, TILE))
    own_base = (own_base[:4] + own_base[4:]).reshape(2, TILE) + own_state.astype(f32)

    squared = jnp.broadcast_to(jnp.sum(grads * grads), (1, 128))
    squared = jnp.sum(share(squared, ("x", "core", "z"), 64), axis=0)
    clip = jnp.minimum(f32(1.0), f32(1.0) / (jnp.sqrt(squared) + 1e-06))
    grads = clip * grads

    def update(values, first, second, slopes):
        moment_one = beta_one * first + (1.0 - beta_one) * slopes
        moment_two = beta_two * second + (1.0 - beta_two) * slopes * slopes
        step_size = (
            moment_one
            / (1.0 - beta_one**adam_count)
            / (jnp.sqrt(moment_two / (1.0 - beta_two**adam_count)) + 1e-08)
        )
        return values - rate * step_size

    own_grads = lax.dynamic_slice_in_dim(grads, y * OWN, OWN, 0)
    updated = update(old[:OWN], old[OWN : 2 * OWN], old[2 * OWN :], own_grads)
    new_factors = lax.ppermute(updated, Y + ("core",), back)[None]

    near = lax.dynamic_slice_in_dim(low, part * TILE, TILE, 0).astype(f32)
    near = update(
        near,
        moments[:, :OWN].reshape(TILE, 128),
        moments[:, OWN:].reshape(TILE, 128),
        grads,
    )
    down = near[:, :RANK].astype(bf16)
    up = near[:, RANK:].astype(bf16).astype(f32).T
    own_gain = lax.dynamic_slice_in_dim(gain, part * TILE, TILE, 0)

    def spread(pair):
        return jnp.broadcast_to(pair[:, None], (2, 64)).reshape(1, 128)

    thin = jnp.dot(own_state, down, preferred_element_type=f32).reshape(1, 128)
    thin = jnp.sum(share(thin, ("x", "core", "z"), 64), axis=0).reshape(2, RANK)
    resid = own_base + scale * jnp.dot(thin, up, precision=HIGHEST)

    for step in range(1, DECODE_STEPS):
        own = (resid * own_gain).astype(bf16)
        thin = jnp.dot(own, down, preferred_element_type=f32).reshape(1, 128)
        pairs = jnp.concatenate([thin, spread(jnp.sum(resid * resid, axis=1))], axis=0)
        sent = jnp.concatenate([own.reshape(4, 128), *high_low(pairs)], axis=0)
        got = share(sent, ("x", "z"), 32).reshape(4, 8, 8, 128)
        current = pick(got[:, :, :4].reshape(4, 4, 2, 2, TILE), x, 1)
        current = current.transpose(2, 1, 0, 3).reshape(2, BLOCK)
        pairs = jnp.sum(got[:, :, 4:].astype(f32), axis=(0, 1))
        pairs = 0.25 * (pairs[:2] + pairs[2:])
        sums = lax.optimization_barrier(jnp.dot(current, rows, preferred_element_type=f32))
        sums = sums.reshape(2, 8, TILE).transpose(1, 0, 2).reshape(8, 4, 128)
        sent = jnp.concatenate([sums, jnp.broadcast_to(pairs[None], (8, 2, 128))], axis=1)
        got = jnp.sum(swap(sent, ("x", "core")), axis=0)
        thin = got[4].reshape(2, RANK)
        norm = lax.rsqrt(got[5].reshape(2, 64)[:, :1] / MODEL_WIDTH + 1e-05)
        total = own.astype(f32) + got[:4].reshape(2, TILE)
        resid = norm * (total + scale * jnp.dot(thin, up, precision=HIGHEST))

    sums = jnp.sum(share(spread(jnp.sum(resid * resid, axis=1)), ("x", "core", "z"), 64), axis=0)
    norm = lax.rsqrt(sums.reshape(2, 64)[:, :1] / MODEL_WIDTH + 1e-05)
    own = (resid * norm * own_gain).astype(bf16)
    result = share(own.reshape(4, 128), DP, 64).reshape(4, 8, 2, 2, TILE)
    result = result.transpose(1, 3, 0, 2, 4).reshape(BATCH, BLOCK)
    return (new_factors, result)


def solution(mesh):
    fine = Mesh(mesh.devices.reshape(4, 2, 2, 2, 2, 8), AXES)
    return jax.shard_map(
        body,
        mesh=fine,
        in_specs=(
            P(DP, "z"),
            P(DP, "z"),
            P(DP),
            P(DP),
            P(DP),
            P("z", DP, None),
            P("z", DP, None),
            P("z", DP, None),
            P(DP, "z"),
            P("z"),
            P(None, "z"),
        ),
        out_specs=(P("z", DP, None), P(None, "z")),
        check_vma=False,
    )
```

```python
import math

import jax
import jax.numpy as jnp
from jax import lax
from jax.sharding import Mesh
from jax.sharding import PartitionSpec as P

MODEL_WIDTH = 16384
SEQLEN = 128
GROUP = 8
DECODE_STEPS = 4
RANK = 64
BATCH = 16
BLOCK = 2048
TILE = 256
OWN = 32

adapter_alpha = 2.0
beta_one = 0.9
beta_two = 0.999
rate = 0.1
adam_count = 200.0
scale = adapter_alpha / (RANK * math.sqrt(MODEL_WIDTH))

bf16 = jnp.bfloat16
f32 = jnp.float32
HIGHEST = lax.Precision.HIGHEST

AXES = ("x", "ya", "yb", "yc", "core", "z")
DP = ("x", "ya", "yb", "yc", "core")
XY = ("x", "ya", "yb", "yc")
MINOR = ("yb", "yc", "core")
CROSS = ("x", "ya", "z")


def swap(chunks, axes):
    return lax.all_to_all(chunks, axes, 0, 0, tiled=False)


def share(piece, axes, count):
    return swap(jnp.broadcast_to(piece[None], (count,) + piece.shape), axes)


def core_swap(value):
    return lax.ppermute(value, "core", [(0, 1), (1, 0)])


def high_low(value):
    high = lax.reduce_precision(value, 8, 7)
    return high.astype(bf16), (value - high).astype(bf16)


def pick(value, index, axis):
    return lax.dynamic_index_in_dim(value, index, axis, keepdims=False)


def body(
    tokens,
    cotangent,
    prompt_len,
    resp_len,
    ranks,
    factors,
    first_moment,
    second_moment,
    base_weight,
    gain,
    state,
):
    core = lax.axis_index("core")
    z = lax.axis_index("z")
    major = lax.axis_index(("x", "ya"))
    minor = lax.axis_index(MINOR)

    panel = lax.all_gather(base_weight, "z", axis=0, tiled=False)

    there = [((k * 8 + i) * 8 + t, (t * 8 + k) * 8 + i) for k in range(8) for i in range(8) for t in range(8)]
    back = [(b, a) for a, b in there]
    old = lax.ppermute(
        jnp.concatenate([factors[0], first_moment[0], second_moment[0]], axis=0), AXES, there
    )

    positions = jnp.arange(SEQLEN, dtype=jnp.int32)
    lower = prompt_len[:, None]
    upper = lower + resp_len[:, None]
    inside = (positions[None, :] >= lower) & (positions[None, :] < upper)
    advantage = (2 * ranks - (GROUP - 1)).astype(f32) / (GROUP - 1)
    per_seq = advantage / resp_len.astype(f32)
    weight = jnp.where(inside, per_seq[:, None], f32(0.0)).reshape(-1)
    weighted = (cotangent.astype(f32) * weight[:, None]).astype(bf16)

    mine = share(factors[0].astype(bf16), XY, 32)
    other = core_swap(mine)
    low = jnp.where(core == 0, jnp.stack([mine, other], 1), jnp.stack([other, mine], 1))
    low = low.reshape(BLOCK, 2 * RANK)
    hidden = jnp.dot(tokens, low[:, :RANK], preferred_element_type=f32)
    projected = jnp.dot(weighted, low[:, RANK:], preferred_element_type=f32)
    state_tile = lax.dynamic_slice_in_dim(state, minor * TILE, TILE, 1)
    tile_gain = lax.dynamic_slice_in_dim(gain, minor * TILE, TILE, 0)
    sent = jnp.concatenate(
        [
            jnp.concatenate([hidden, projected], axis=1).astype(bf16),
            state_tile.reshape(32, 128),
            *[part.reshape(2, 128) for part in high_low(tile_gain)],
        ],
        axis=0,
    )
    got = share(sent, "z", 8)
    both = jnp.sum(got[:, :SEQLEN].astype(f32), axis=0).astype(bf16)
    home = pick(got[:, SEQLEN:], major, 0)
    first = home[:32].reshape(BATCH, TILE)
    tile_gain = home[32:].astype(f32)
    tile_gain = (tile_gain[:2] + tile_gain[2:]).reshape(TILE)
    own_state = lax.dynamic_slice_in_dim(first, 2 * z, 2, 0)

    dims = (((0,), (0,)), ((), ()))
    grad_down = lax.dot_general(tokens, both[:, RANK:], dims, preferred_element_type=f32)
    grad_up = lax.dot_general(weighted, both[:, :RANK], dims, preferred_element_type=f32)
    grads = jnp.concatenate([grad_down, grad_up], axis=1).astype(bf16).reshape(8, TILE, 128)
    first = jnp.dot(first, base_weight, preferred_element_type=f32)
    first = first.reshape(BATCH, 8, TILE).transpose(1, 0, 2).reshape(8, 32, 128)
    got = swap(jnp.concatenate([grads, *high_low(first)], axis=1), MINOR).astype(f32)
    got = jnp.sum(got, axis=0)
    first = got[TILE : TILE + 32] + got[TILE + 32 :]
    got = lax.ppermute(
        jnp.concatenate([got[:TILE].astype(bf16), *high_low(first)], axis=0),
        CROSS,
        [(k * 8 + t, t * 8 + k) for k in range(8) for t in range(8)],
    )
    rows = jnp.concatenate([got[:TILE], old.astype(bf16)], axis=0)
    rows = jnp.broadcast_to(rows[None], (8, TILE + 3 * OWN, 128))
    first = [got[TILE : TILE + 32].reshape(8, 4, 128), got[TILE + 32 :].reshape(8, 4, 128)]
    got = swap(jnp.concatenate([rows, *first], axis=1), "z").astype(f32)
    grads = scale * jnp.sum(got[:, :TILE], axis=0)
    former = got[:, TILE : TILE + 3 * OWN]
    base = jnp.sum(got[:, TILE + 3 * OWN :], axis=0)
    base = (base[:4] + base[4:]).reshape(2, TILE) + own_state.astype(f32)

    squared = jnp.broadcast_to(jnp.sum(grads * grads), (1, 128))
    squared = jnp.sum(share(squared, DP, 64), axis=0)
    clip = jnp.minimum(f32(1.0), f32(1.0) / (jnp.sqrt(squared) + 1e-06))
    grads = clip * grads

    def update(values, first, second, slopes):
        moment_one = beta_one * first + (1.0 - beta_one) * slopes
        moment_two = beta_two * second + (1.0 - beta_two) * slopes * slopes
        step_size = (
            moment_one
            / (1.0 - beta_one**adam_count)
            / (jnp.sqrt(moment_two / (1.0 - beta_two**adam_count)) + 1e-08)
        )
        return values - rate * step_size

    own_grads = lax.dynamic_slice_in_dim(grads, z * OWN, OWN, 0)
    updated = update(old[:OWN], old[OWN : 2 * OWN], old[2 * OWN :], own_grads)
    new_factors = lax.ppermute(updated, AXES, back)[None]

    near = update(
        former[:, :OWN].reshape(TILE, 128),
        former[:, OWN : 2 * OWN].reshape(TILE, 128),
        former[:, 2 * OWN :].reshape(TILE, 128),
        grads,
    )
    down = near[:, :RANK].astype(bf16)
    up = near[:, RANK:].astype(bf16).astype(f32).T

    thin = jnp.dot(own_state, down, preferred_element_type=f32).reshape(1, 128)
    thin = jnp.sum(share(thin, DP, 64), axis=0).reshape(2, RANK)
    resid = base + scale * jnp.dot(thin, up, precision=HIGHEST)

    def packed(sums):
        halves = [jnp.broadcast_to(half[:, None], (2, 32)) for half in high_low(sums)]
        return jnp.concatenate(halves, axis=1).reshape(1, 128)

    for step in range(1, DECODE_STEPS):
        own = (resid * tile_gain).astype(bf16)
        thin = jnp.dot(own, down, preferred_element_type=f32).astype(bf16).reshape(1, 128)
        extra = jnp.concatenate([thin, packed(jnp.sum(resid * resid, axis=1))], axis=0)
        sums = jnp.einsum(
            "zsk,zkn->zsn",
            jnp.broadcast_to(own[None], (8, 2, TILE)),
            panel,
            preferred_element_type=f32,
        )
        sums = lax.optimization_barrier(sums.astype(bf16))
        sums = sums.reshape(8, 2, 8, TILE).transpose(0, 2, 1, 3).reshape(64, 4, 128)
        sent = jnp.concatenate([sums, jnp.broadcast_to(extra[None], (64, 2, 128))], axis=1)
        got = jnp.sum(swap(sent, DP).astype(f32), axis=0)
        thin = got[4].reshape(2, RANK)
        squares = got[5].reshape(2, 2, 32)[:, :, 0]
        norm = lax.rsqrt((squares[:, :1] + squares[:, 1:]) / MODEL_WIDTH + 1e-05)
        total = own.astype(f32) + got[:4].reshape(2, TILE)
        resid = norm * (total + scale * jnp.dot(thin, up, precision=HIGHEST))

    own = (resid * tile_gain).astype(bf16).reshape(4, 128)
    sent = jnp.concatenate([own, packed(jnp.sum(resid * resid, axis=1))], axis=0)
    got = share(sent, CROSS, 64).reshape(8, 8, 5, 128)
    sums = jnp.sum(got[:, :, 4].astype(f32), axis=0).reshape(BATCH, 2, 32)[:, :, :8]
    sums = (sums[:, 0] + sums[:, 1]).reshape(1, 128)
    sent = jnp.concatenate([pick(got[:, :, :4], z, 0).reshape(32, 128), *high_low(sums)], axis=0)
    got = share(sent, MINOR, 8)
    sums = jnp.sum(got[:, 32:].astype(f32), axis=(0, 1)).reshape(BATCH, 8)[:, :1]
    norm = lax.rsqrt(sums / MODEL_WIDTH + 1e-05)
    result = got[:, :32].reshape(8, BATCH, TILE).transpose(1, 0, 2).reshape(BATCH, BLOCK)
    result = (result.astype(f32) * norm).astype(bf16)
    return (new_factors, result)


def solution(mesh):
    fine = Mesh(mesh.devices.reshape(4, 2, 2, 2, 2, 8), AXES)
    return jax.shard_map(
        body,
        mesh=fine,
        in_specs=(
            P(DP, "z"),
            P(DP, "z"),
            P(DP),
            P(DP),
            P(DP),
            P("z", DP, None),
            P("z", DP, None),
            P("z", DP, None),
            P(DP, "z"),
            P("z"),
            P(None, "z"),
        ),
        out_specs=(P("z", DP, None), P(None, "z")),
        check_vma=False,
    )
```

```python
import math

import jax
import jax.numpy as jnp
from jax import lax
from jax.sharding import Mesh
from jax.sharding import PartitionSpec as P

MODEL_WIDTH = 16384
SEQLEN = 128
GROUP = 8
DECODE_STEPS = 4
RANK = 64
BATCH = 16
BLOCK = 2048
TILE = 256
OWN = 32

adapter_alpha = 2.0
beta_one = 0.9
beta_two = 0.999
rate = 0.1
adam_count = 200.0
scale = adapter_alpha / (RANK * math.sqrt(MODEL_WIDTH))

bf16 = jnp.bfloat16
f32 = jnp.float32
HIGHEST = lax.Precision.HIGHEST

AXES = ("x", "ya", "yb", "yc", "core", "z")
DP = ("x", "ya", "yb", "yc", "core")
XY = ("x", "ya", "yb", "yc")
MINOR = ("yb", "yc", "core")
CROSS = ("x", "ya", "z")


def swap(chunks, axes):
    return lax.all_to_all(chunks, axes, 0, 0, tiled=False)


def share(piece, axes, count):
    return swap(jnp.broadcast_to(piece[None], (count,) + piece.shape), axes)


def core_swap(value):
    return lax.ppermute(value, "core", [(0, 1), (1, 0)])


def high_low(value):
    high = lax.reduce_precision(value, 8, 7)
    return high.astype(bf16), (value - high).astype(bf16)


def pick(value, index, axis):
    return lax.dynamic_index_in_dim(value, index, axis, keepdims=False)


def body(
    tokens,
    cotangent,
    prompt_len,
    resp_len,
    ranks,
    factors,
    first_moment,
    second_moment,
    base_weight,
    gain,
    state,
):
    core = lax.axis_index("core")
    z = lax.axis_index("z")
    major = lax.axis_index(("x", "ya"))
    minor = lax.axis_index(MINOR)

    panel = lax.all_gather(base_weight, "z", axis=0, tiled=False)

    there = [((k * 8 + i) * 8 + t, (t * 8 + k) * 8 + i) for k in range(8) for i in range(8) for t in range(8)]
    back = [(b, a) for a, b in there]
    old = lax.ppermute(
        jnp.concatenate([factors[0], first_moment[0], second_moment[0]], axis=0), AXES, there
    )

    positions = jnp.arange(SEQLEN, dtype=jnp.int32)
    lower = prompt_len[:, None]
    upper = lower + resp_len[:, None]
    inside = (positions[None, :] >= lower) & (positions[None, :] < upper)
    advantage = (2 * ranks - (GROUP - 1)).astype(f32) / (GROUP - 1)
    per_seq = advantage / resp_len.astype(f32)
    weight = jnp.where(inside, per_seq[:, None], f32(0.0)).reshape(-1)
    weighted = (cotangent.astype(f32) * weight[:, None]).astype(bf16)

    mine = share(factors[0].astype(bf16), XY, 32)
    mine, old = lax.optimization_barrier((mine, old))
    other = core_swap(mine)
    low = jnp.where(core == 0, jnp.stack([mine, other], 1), jnp.stack([other, mine], 1))
    low = low.reshape(BLOCK, 2 * RANK)
    hidden = jnp.dot(tokens, low[:, :RANK], preferred_element_type=f32)
    projected = jnp.dot(weighted, low[:, RANK:], preferred_element_type=f32)
    state_tile = lax.dynamic_slice_in_dim(state, minor * TILE, TILE, 1)
    tile_gain = lax.dynamic_slice_in_dim(gain, minor * TILE, TILE, 0)
    sent = jnp.concatenate(
        [
            jnp.concatenate([hidden, projected], axis=1).astype(bf16),
            state_tile.reshape(32, 128),
            *[part.reshape(2, 128) for part in high_low(tile_gain)],
        ],
        axis=0,
    )
    got = share(sent, "z", 8)
    both = jnp.sum(got[:, :SEQLEN].astype(f32), axis=0).astype(bf16)
    home = pick(got[:, SEQLEN:], major, 0)
    first = home[:32].reshape(BATCH, TILE)
    tile_gain = home[32:].astype(f32)
    tile_gain = (tile_gain[:2] + tile_gain[2:]).reshape(TILE)
    own_state = lax.dynamic_slice_in_dim(first, 2 * z, 2, 0)

    dims = (((0,), (0,)), ((), ()))
    grad_down = lax.dot_general(tokens, both[:, RANK:], dims, preferred_element_type=f32)
    grad_up = lax.dot_general(weighted, both[:, :RANK], dims, preferred_element_type=f32)
    grads = jnp.concatenate([grad_down, grad_up], axis=1).astype(bf16).reshape(4, 2, 8, OWN, 128)
    first = jnp.dot(first, base_weight, preferred_element_type=f32)
    first = first.reshape(8, 2, 4, 2, TILE)

    def half(which):
        base = pick(first, which, 3).transpose(0, 2, 1, 3).reshape(32, 4, 128)
        return pick(grads, which, 1).transpose(1, 0, 2, 3).reshape(32, OWN, 128), base

    give, give_base = half(1 - core)
    keep, keep_base = half(core)
    got = core_swap(jnp.concatenate([give, *high_low(give_base)], axis=1)).astype(f32)
    keep = (keep.astype(f32) + got[:, :OWN]).astype(bf16)
    keep_base = keep_base + got[:, OWN : OWN + 4] + got[:, OWN + 4 :]
    got = swap(jnp.concatenate([keep, *high_low(keep_base)], axis=1), XY).astype(f32)
    got = jnp.sum(got, axis=0)
    base = got[OWN : OWN + 4] + got[OWN + 4 :]
    got = lax.ppermute(
        jnp.concatenate([got[:OWN].astype(bf16), *high_low(base)], axis=0),
        CROSS,
        [(k * 8 + t, t * 8 + k) for k in range(8) for t in range(8)],
    )
    base = (got[OWN : OWN + 4].astype(f32) + got[OWN + 4 :].astype(f32)).reshape(2, TILE)
    base = base + own_state.astype(f32)
    got = share(jnp.concatenate([got[:OWN], old.astype(bf16)], axis=0), "z", 8).astype(f32)
    grads = scale * got[:, :OWN].reshape(TILE, 128)
    former = got[:, OWN:]

    squared = jnp.broadcast_to(jnp.sum(grads * grads), (1, 128))
    squared = jnp.sum(share(squared, DP, 64), axis=0)
    clip = jnp.minimum(f32(1.0), f32(1.0) / (jnp.sqrt(squared) + 1e-06))
    grads = clip * grads

    def update(values, first, second, slopes):
        moment_one = beta_one * first + (1.0 - beta_one) * slopes
        moment_two = beta_two * second + (1.0 - beta_two) * slopes * slopes
        step_size = (
            moment_one
            / (1.0 - beta_one**adam_count)
            / (jnp.sqrt(moment_two / (1.0 - beta_two**adam_count)) + 1e-08)
        )
        return values - rate * step_size

    own_grads = lax.dynamic_slice_in_dim(grads, z * OWN, OWN, 0)
    updated = update(old[:OWN], old[OWN : 2 * OWN], old[2 * OWN :], own_grads)
    new_factors = lax.ppermute(updated, AXES, back)[None]

    near = update(
        former[:, :OWN].reshape(TILE, 128),
        former[:, OWN : 2 * OWN].reshape(TILE, 128),
        former[:, 2 * OWN :].reshape(TILE, 128),
        grads,
    )
    down = near[:, :RANK].astype(bf16)
    up = near[:, RANK:].astype(bf16).astype(f32).T

    thin = jnp.dot(own_state, down, preferred_element_type=f32).reshape(1, 128)
    thin = jnp.sum(share(thin, DP, 64), axis=0).reshape(2, RANK)
    resid = base + scale * jnp.dot(thin, up, precision=HIGHEST)

    def packed(sums):
        halves = [jnp.broadcast_to(half[:, None], (2, 32)) for half in high_low(sums)]
        return jnp.concatenate(halves, axis=1).reshape(1, 128)

    for step in range(1, DECODE_STEPS):
        own = (resid * tile_gain).astype(bf16)
        thin = jnp.dot(own, down, preferred_element_type=f32).astype(bf16).reshape(1, 128)
        extra = jnp.concatenate([thin, packed(jnp.sum(resid * resid, axis=1))], axis=0)
        sums = jnp.einsum(
            "zsk,zkn->zsn",
            jnp.broadcast_to(own[None], (8, 2, TILE)),
            panel,
            preferred_element_type=f32,
        )
        sums = lax.optimization_barrier(sums.astype(bf16))
        sums = sums.reshape(8, 2, 8, TILE).transpose(0, 2, 1, 3).reshape(64, 4, 128)
        sent = jnp.concatenate([sums, jnp.broadcast_to(extra[None], (64, 2, 128))], axis=1)
        got = jnp.sum(swap(sent, DP).astype(f32), axis=0)
        if step == 1:
            got, new_factors = lax.optimization_barrier((got, new_factors))
        thin = got[4].reshape(2, RANK)
        squares = got[5].reshape(2, 2, 32)[:, :, 0]
        norm = lax.rsqrt((squares[:, :1] + squares[:, 1:]) / MODEL_WIDTH + 1e-05)
        total = own.astype(f32) + got[:4].reshape(2, TILE)
        resid = norm * (total + scale * jnp.dot(thin, up, precision=HIGHEST))

    own = (resid * tile_gain).astype(bf16).reshape(4, 128)
    sent = jnp.concatenate([own, packed(jnp.sum(resid * resid, axis=1))], axis=0)
    got = share(sent, CROSS, 64).reshape(8, 8, 5, 128)
    sums = jnp.sum(got[:, :, 4].astype(f32), axis=0).reshape(BATCH, 2, 32)[:, :, :8]
    sums = (sums[:, 0] + sums[:, 1]).reshape(1, 128)
    sent = jnp.concatenate([pick(got[:, :, :4], z, 0).reshape(32, 128), *high_low(sums)], axis=0)
    got = share(sent, MINOR, 8)
    sums = jnp.sum(got[:, 32:].astype(f32), axis=(0, 1)).reshape(BATCH, 8)[:, :1]
    norm = lax.rsqrt(sums / MODEL_WIDTH + 1e-05)
    result = got[:, :32].reshape(8, BATCH, TILE).transpose(1, 0, 2).reshape(BATCH, BLOCK)
    result = (result.astype(f32) * norm).astype(bf16)
    return (new_factors, result)


def solution(mesh):
    fine = Mesh(mesh.devices.reshape(4, 2, 2, 2, 2, 8), AXES)
    return jax.shard_map(
        body,
        mesh=fine,
        in_specs=(
            P(DP, "z"),
            P(DP, "z"),
            P(DP),
            P(DP),
            P(DP),
            P("z", DP, None),
            P("z", DP, None),
            P("z", DP, None),
            P(DP, "z"),
            P("z"),
            P(None, "z"),
        ),
        out_specs=(P("z", DP, None), P(None, "z")),
        check_vma=False,
    )
```

```python
import math

import jax
import jax.numpy as jnp
from jax import lax
from jax.sharding import Mesh
from jax.sharding import PartitionSpec as P

MODEL_WIDTH = 16384
SEQLEN = 128
GROUP = 8
DECODE_STEPS = 4
RANK = 64
BATCH = 16
BLOCK = 2048
TILE = 256
OWN = 32

adapter_alpha = 2.0
beta_one = 0.9
beta_two = 0.999
rate = 0.1
adam_count = 200.0
scale = adapter_alpha / (RANK * math.sqrt(MODEL_WIDTH))

bf16 = jnp.bfloat16
f32 = jnp.float32
HIGHEST = lax.Precision.HIGHEST

AXES = ("x", "ya", "yb", "yc", "core", "z")
DP = ("x", "ya", "yb", "yc", "core")
XY = ("x", "ya", "yb", "yc")
MINOR = ("yb", "yc", "core")
CROSS = ("x", "ya", "z")


def swap(chunks, axes):
    return lax.all_to_all(chunks, axes, 0, 0, tiled=False)


def share(piece, axes, count):
    return swap(jnp.broadcast_to(piece[None], (count,) + piece.shape), axes)


def core_swap(value):
    return lax.ppermute(value, "core", [(0, 1), (1, 0)])


def high_low(value):
    high = lax.reduce_precision(value, 8, 7)
    return high.astype(bf16), (value - high).astype(bf16)


def pick(value, index, axis):
    return lax.dynamic_index_in_dim(value, index, axis, keepdims=False)


def body(
    tokens,
    cotangent,
    prompt_len,
    resp_len,
    ranks,
    factors,
    first_moment,
    second_moment,
    base_weight,
    gain,
    state,
):
    core = lax.axis_index("core")
    z = lax.axis_index("z")
    major = lax.axis_index(("x", "ya"))
    minor = lax.axis_index(MINOR)

    panel = lax.all_gather(base_weight, "z", axis=0, tiled=False)

    positions = jnp.arange(SEQLEN, dtype=jnp.int32)
    lower = prompt_len[:, None]
    upper = lower + resp_len[:, None]
    inside = (positions[None, :] >= lower) & (positions[None, :] < upper)
    advantage = (2 * ranks - (GROUP - 1)).astype(f32) / (GROUP - 1)
    per_seq = advantage / resp_len.astype(f32)
    weight = jnp.where(inside, per_seq[:, None], f32(0.0)).reshape(-1)
    weighted = (cotangent.astype(f32) * weight[:, None]).astype(bf16)

    mine = share(factors[0].astype(bf16), XY, 32)
    other = core_swap(mine)
    low = jnp.where(core == 0, jnp.stack([mine, other], 1), jnp.stack([other, mine], 1))
    low = low.reshape(BLOCK, 2 * RANK)
    hidden = jnp.dot(tokens, low[:, :RANK], preferred_element_type=f32)
    projected = jnp.dot(weighted, low[:, RANK:], preferred_element_type=f32)
    state_tile = lax.dynamic_slice_in_dim(state, minor * TILE, TILE, 1)
    tile_gain = lax.dynamic_slice_in_dim(gain, minor * TILE, TILE, 0)
    sent = jnp.concatenate(
        [
            jnp.concatenate([hidden, projected], axis=1).astype(bf16),
            state_tile.reshape(32, 128),
            *[part.reshape(2, 128) for part in high_low(tile_gain)],
        ],
        axis=0,
    )
    got = share(sent, "z", 8)
    both = jnp.sum(got[:, :SEQLEN].astype(f32), axis=0).astype(bf16)
    home = pick(got[:, SEQLEN:], major, 0)
    first = home[:32].reshape(BATCH, TILE)
    tile_gain = home[32:].astype(f32)
    tile_gain = (tile_gain[:2] + tile_gain[2:]).reshape(TILE)
    own_state = lax.dynamic_slice_in_dim(first, 2 * z, 2, 0)

    dims = (((0,), (0,)), ((), ()))
    grad_down = lax.dot_general(tokens, both[:, RANK:], dims, preferred_element_type=f32)
    grad_up = lax.dot_general(weighted, both[:, :RANK], dims, preferred_element_type=f32)
    grads = jnp.concatenate([grad_down, grad_up], axis=1).astype(bf16).reshape(32, 2, OWN, 128)
    first = jnp.dot(first, base_weight, preferred_element_type=f32)
    first = first.reshape(4, 2, 2, 8, TILE)

    def half(which):
        base = pick(first, which, 1).transpose(2, 0, 1, 3).reshape(32, 4, 128)
        return pick(grads, which, 1), base

    give, give_base = half(1 - core)
    keep, keep_base = half(core)
    got = core_swap(jnp.concatenate([give, *high_low(give_base)], axis=1)).astype(f32)
    keep = (keep.astype(f32) + got[:, :OWN]).astype(bf16)
    keep_base = keep_base + got[:, OWN : OWN + 4] + got[:, OWN + 4 :]
    got = swap(jnp.concatenate([keep, *high_low(keep_base)], axis=1), XY).astype(f32)
    got = jnp.sum(got, axis=0)
    base = got[OWN : OWN + 4] + got[OWN + 4 :]
    own_grads = got[:OWN]
    old = jnp.concatenate([factors[0], first_moment[0], second_moment[0]], axis=0)
    got = lax.ppermute(
        jnp.concatenate([own_grads.astype(bf16), old.astype(bf16), *high_low(base)], axis=0),
        AXES,
        [((k * 8 + i) * 8 + t, (t * 8 + k) * 8 + i) for k in range(8) for i in range(8) for t in range(8)],
    )
    base = (got[4 * OWN : 4 * OWN + 4].astype(f32) + got[4 * OWN + 4 :].astype(f32)).reshape(2, TILE)
    base = base + own_state.astype(f32)
    got = share(got[: 4 * OWN], "z", 8).astype(f32)
    grads = scale * got[:, :OWN].reshape(TILE, 128)
    former = got[:, OWN:]

    squared = jnp.broadcast_to(jnp.sum(grads * grads), (1, 128))
    squared = jnp.sum(share(squared, DP, 64), axis=0)
    clip = jnp.minimum(f32(1.0), f32(1.0) / (jnp.sqrt(squared) + 1e-06))
    grads = clip * grads

    def update(values, first, second, slopes):
        moment_one = beta_one * first + (1.0 - beta_one) * slopes
        moment_two = beta_two * second + (1.0 - beta_two) * slopes * slopes
        step_size = (
            moment_one
            / (1.0 - beta_one**adam_count)
            / (jnp.sqrt(moment_two / (1.0 - beta_two**adam_count)) + 1e-08)
        )
        return values - rate * step_size

    own_grads = clip * (scale * own_grads)
    new_factors = update(factors[0], first_moment[0], second_moment[0], own_grads)[None]

    near = update(
        former[:, :OWN].reshape(TILE, 128),
        former[:, OWN : 2 * OWN].reshape(TILE, 128),
        former[:, 2 * OWN :].reshape(TILE, 128),
        grads,
    )
    down = near[:, :RANK].astype(bf16)
    up = near[:, RANK:].astype(bf16).astype(f32).T

    thin = jnp.dot(own_state, down, preferred_element_type=f32).reshape(1, 128)
    thin = jnp.sum(share(thin, DP, 64), axis=0).reshape(2, RANK)
    resid = base + scale * jnp.dot(thin, up, precision=HIGHEST)

    def packed(sums):
        halves = [jnp.broadcast_to(half[:, None], (2, 32)) for half in high_low(sums)]
        return jnp.concatenate(halves, axis=1).reshape(1, 128)

    for step in range(1, DECODE_STEPS):
        own = (resid * tile_gain).astype(bf16)
        thin = jnp.dot(own, down, preferred_element_type=f32).astype(bf16).reshape(1, 128)
        extra = jnp.concatenate([thin, packed(jnp.sum(resid * resid, axis=1))], axis=0)
        sums = jnp.einsum(
            "zsk,zkn->zsn",
            jnp.broadcast_to(own[None], (8, 2, TILE)),
            panel,
            preferred_element_type=f32,
        )
        sums = lax.optimization_barrier(sums.astype(bf16))
        sums = sums.reshape(8, 2, 8, TILE).transpose(0, 2, 1, 3).reshape(64, 4, 128)
        sent = jnp.concatenate([sums, jnp.broadcast_to(extra[None], (64, 2, 128))], axis=1)
        got = jnp.sum(swap(sent, DP).astype(f32), axis=0)
        thin = got[4].reshape(2, RANK)
        squares = got[5].reshape(2, 2, 32)[:, :, 0]
        norm = lax.rsqrt((squares[:, :1] + squares[:, 1:]) / MODEL_WIDTH + 1e-05)
        total = own.astype(f32) + got[:4].reshape(2, TILE)
        resid = norm * (total + scale * jnp.dot(thin, up, precision=HIGHEST))

    own = (resid * tile_gain).astype(bf16).reshape(4, 128)
    sent = jnp.concatenate([own, packed(jnp.sum(resid * resid, axis=1))], axis=0)
    got = share(sent, CROSS, 64).reshape(8, 8, 5, 128)
    sums = jnp.sum(got[:, :, 4].astype(f32), axis=0).reshape(BATCH, 2, 32)[:, :, :8]
    sums = (sums[:, 0] + sums[:, 1]).reshape(1, 128)
    sent = jnp.concatenate([pick(got[:, :, :4], z, 0).reshape(32, 128), *high_low(sums)], axis=0)
    got = share(sent, MINOR, 8)
    sums = jnp.sum(got[:, 32:].astype(f32), axis=(0, 1)).reshape(BATCH, 8)[:, :1]
    norm = lax.rsqrt(sums / MODEL_WIDTH + 1e-05)
    result = got[:, :32].reshape(8, BATCH, TILE).transpose(1, 0, 2).reshape(BATCH, BLOCK)
    result = (result.astype(f32) * norm).astype(bf16)
    return (new_factors, result)


def solution(mesh):
    fine = Mesh(mesh.devices.reshape(4, 2, 2, 2, 2, 8), AXES)
    return jax.shard_map(
        body,
        mesh=fine,
        in_specs=(
            P(DP, "z"),
            P(DP, "z"),
            P(DP),
            P(DP),
            P(DP),
            P("z", DP, None),
            P("z", DP, None),
            P("z", DP, None),
            P(DP, "z"),
            P("z"),
            P(None, "z"),
        ),
        out_specs=(P("z", DP, None), P(None, "z")),
        check_vma=False,
    )
```

```python
import math

import jax
import jax.numpy as jnp
from jax import lax
from jax.sharding import Mesh
from jax.sharding import PartitionSpec as P

MODEL_WIDTH = 16384
SEQLEN = 128
GROUP = 8
DECODE_STEPS = 4
RANK = 64
BATCH = 16
BLOCK = 2048
TILE = 256
OWN = 32

adapter_alpha = 2.0
beta_one = 0.9
beta_two = 0.999
rate = 0.1
adam_count = 200.0
scale = adapter_alpha / (RANK * math.sqrt(MODEL_WIDTH))

bf16 = jnp.bfloat16
f32 = jnp.float32
HIGHEST = lax.Precision.HIGHEST

AXES = ("x", "ya", "yb", "yc", "core", "z")
DP = ("x", "ya", "yb", "yc", "core")
XY = ("x", "ya", "yb", "yc")
MINOR = ("yb", "yc", "core")
CROSS = ("x", "ya", "z")


def swap(chunks, axes):
    return lax.all_to_all(chunks, axes, 0, 0, tiled=False)


def share(piece, axes, count):
    return swap(jnp.broadcast_to(piece[None], (count,) + piece.shape), axes)


def core_swap(value):
    return lax.ppermute(value, "core", [(0, 1), (1, 0)])


def high_low(value):
    high = lax.reduce_precision(value, 8, 7)
    return high.astype(bf16), (value - high).astype(bf16)


def pick(value, index, axis):
    return lax.dynamic_index_in_dim(value, index, axis, keepdims=False)


def body(
    tokens,
    cotangent,
    prompt_len,
    resp_len,
    ranks,
    factors,
    first_moment,
    second_moment,
    base_weight,
    gain,
    state,
):
    core = lax.axis_index("core")
    z = lax.axis_index("z")
    major = lax.axis_index(("x", "ya"))
    minor = lax.axis_index(MINOR)

    panel = lax.all_gather(base_weight, "z", axis=0, tiled=False)

    positions = jnp.arange(SEQLEN, dtype=jnp.int32)
    lower = prompt_len[:, None]
    upper = lower + resp_len[:, None]
    inside = (positions[None, :] >= lower) & (positions[None, :] < upper)
    advantage = (2 * ranks - (GROUP - 1)).astype(f32) / (GROUP - 1)
    per_seq = advantage / resp_len.astype(f32)
    weight = jnp.where(inside, per_seq[:, None], f32(0.0)).reshape(-1)
    weighted = (cotangent.astype(f32) * weight[:, None]).astype(bf16)
    weighted = lax.optimization_barrier(weighted)

    mine = share(factors[0].astype(bf16), XY, 32)
    other = core_swap(mine)
    low = jnp.where(core == 0, jnp.stack([mine, other], 1), jnp.stack([other, mine], 1))
    low = low.reshape(BLOCK, 2 * RANK)
    hidden = jnp.dot(tokens, low[:, :RANK], preferred_element_type=f32)
    projected = jnp.dot(weighted, low[:, RANK:], preferred_element_type=f32)
    state_tile = lax.dynamic_slice_in_dim(state, minor * TILE, TILE, 1)
    tile_gain = lax.dynamic_slice_in_dim(gain, minor * TILE, TILE, 0)
    sent = jnp.concatenate(
        [
            jnp.concatenate([hidden, projected], axis=1).astype(bf16),
            state_tile.reshape(32, 128),
            *[part.reshape(2, 128) for part in high_low(tile_gain)],
        ],
        axis=0,
    )
    got = share(sent, "z", 8)
    both = jnp.sum(got[:, :SEQLEN].astype(f32), axis=0).astype(bf16)
    home = pick(got[:, SEQLEN:], major, 0)
    first = home[:32].reshape(BATCH, TILE)
    tile_gain = home[32:].astype(f32)
    tile_gain = (tile_gain[:2] + tile_gain[2:]).reshape(TILE)
    own_state = lax.dynamic_slice_in_dim(first, 2 * z, 2, 0)

    dims = (((0,), (0,)), ((), ()))
    grad_down = lax.dot_general(tokens, both[:, RANK:], dims, preferred_element_type=f32)
    grad_up = lax.dot_general(weighted, both[:, :RANK], dims, preferred_element_type=f32)
    grads = jnp.concatenate([grad_down, grad_up], axis=1).astype(bf16).reshape(32, 2, OWN, 128)
    first = jnp.dot(first, base_weight, preferred_element_type=f32)
    first = first.reshape(4, 2, 2, 8, TILE)

    def half(which):
        base = pick(first, which, 1).transpose(2, 0, 1, 3).reshape(32, 4, 128)
        return pick(grads, which, 1), base

    give, give_base = half(1 - core)
    keep, keep_base = half(core)
    got = core_swap(jnp.concatenate([give, *high_low(give_base)], axis=1)).astype(f32)
    keep = (keep.astype(f32) + got[:, :OWN]).astype(bf16)
    keep_base = keep_base + got[:, OWN : OWN + 4] + got[:, OWN + 4 :]
    got = swap(jnp.concatenate([keep, *high_low(keep_base)], axis=1), XY).astype(f32)
    got = jnp.sum(got, axis=0)
    base = got[OWN : OWN + 4] + got[OWN + 4 :]
    own_grads = got[:OWN]
    old = jnp.concatenate([factors[0], first_moment[0], second_moment[0]], axis=0)
    got = lax.ppermute(
        jnp.concatenate([own_grads.astype(bf16), old.astype(bf16), *high_low(base)], axis=0),
        AXES,
        [((k * 8 + i) * 8 + t, (t * 8 + k) * 8 + i) for k in range(8) for i in range(8) for t in range(8)],
    )
    base = (got[4 * OWN : 4 * OWN + 4].astype(f32) + got[4 * OWN + 4 :].astype(f32)).reshape(2, TILE)
    base = base + own_state.astype(f32)
    own_grads = scale * own_grads
    squared = jnp.broadcast_to(jnp.sum(own_grads * own_grads), (1, 128))
    squared = jnp.sum(share(squared, DP, 64), axis=0)
    got = share(jnp.concatenate([got[: 4 * OWN], *high_low(squared)], axis=0), "z", 8).astype(f32)
    grads = scale * got[:, :OWN].reshape(TILE, 128)
    former = got[:, OWN : 4 * OWN]
    squared = jnp.sum(got[:, 4 * OWN :], axis=(0, 1))[None]

    clip = jnp.minimum(f32(1.0), f32(1.0) / (jnp.sqrt(squared) + 1e-06))
    grads = clip * grads

    def update(values, first, second, slopes):
        moment_one = beta_one * first + (1.0 - beta_one) * slopes
        moment_two = beta_two * second + (1.0 - beta_two) * slopes * slopes
        step_size = (
            moment_one
            / (1.0 - beta_one**adam_count)
            / (jnp.sqrt(moment_two / (1.0 - beta_two**adam_count)) + 1e-08)
        )
        return values - rate * step_size

    own_grads = clip * own_grads
    new_factors = update(factors[0], first_moment[0], second_moment[0], own_grads)[None]

    near = update(
        former[:, :OWN].reshape(TILE, 128),
        former[:, OWN : 2 * OWN].reshape(TILE, 128),
        former[:, 2 * OWN :].reshape(TILE, 128),
        grads,
    )
    down = near[:, :RANK].astype(bf16)
    up = near[:, RANK:].astype(bf16).astype(f32).T

    thin = jnp.dot(own_state, down, preferred_element_type=f32).reshape(1, 128)
    thin = jnp.sum(share(thin, DP, 64), axis=0).reshape(2, RANK)
    resid = base + scale * jnp.dot(thin, up, precision=HIGHEST)

    def packed(sums):
        halves = [jnp.broadcast_to(half[:, None], (2, 32)) for half in high_low(sums)]
        return jnp.concatenate(halves, axis=1).reshape(1, 128)

    for step in range(1, DECODE_STEPS):
        own = (resid * tile_gain).astype(bf16)
        thin = jnp.dot(own, down, preferred_element_type=f32).astype(bf16).reshape(1, 128)
        extra = jnp.concatenate([thin, packed(jnp.sum(resid * resid, axis=1))], axis=0)
        sums = jnp.einsum(
            "zsk,zkn->zsn",
            jnp.broadcast_to(own[None], (8, 2, TILE)),
            panel,
            preferred_element_type=f32,
        )
        sums = lax.optimization_barrier(sums.astype(bf16))
        sums = sums.reshape(8, 2, 8, TILE).transpose(0, 2, 1, 3).reshape(64, 4, 128)
        sent = jnp.concatenate([sums, jnp.broadcast_to(extra[None], (64, 2, 128))], axis=1)
        got = jnp.sum(swap(sent, DP).astype(f32), axis=0)
        thin = got[4].reshape(2, RANK)
        squares = got[5].reshape(2, 2, 32)[:, :, 0]
        norm = lax.rsqrt((squares[:, :1] + squares[:, 1:]) / MODEL_WIDTH + 1e-05)
        total = own.astype(f32) + got[:4].reshape(2, TILE)
        resid = norm * (total + scale * jnp.dot(thin, up, precision=HIGHEST))

    own = (resid * tile_gain).astype(bf16).reshape(4, 128)
    sent = jnp.concatenate([own, packed(jnp.sum(resid * resid, axis=1))], axis=0)
    got = share(sent, CROSS, 64).reshape(8, 8, 5, 128)
    sums = jnp.sum(got[:, :, 4].astype(f32), axis=0).reshape(BATCH, 2, 32)[:, :, :8]
    sums = (sums[:, 0] + sums[:, 1]).reshape(1, 128)
    sent = jnp.concatenate([pick(got[:, :, :4], z, 0).reshape(32, 128), *high_low(sums)], axis=0)
    got = share(sent, MINOR, 8)
    sums = jnp.sum(got[:, 32:].astype(f32), axis=(0, 1)).reshape(BATCH, 8)[:, :1]
    norm = lax.rsqrt(sums / MODEL_WIDTH + 1e-05)
    result = got[:, :32].reshape(8, BATCH, TILE).transpose(1, 0, 2).reshape(BATCH, BLOCK)
    result = (result.astype(f32) * norm).astype(bf16)
    return (new_factors, result)


def solution(mesh):
    fine = Mesh(mesh.devices.reshape(4, 2, 2, 2, 2, 8), AXES)
    return jax.shard_map(
        body,
        mesh=fine,
        in_specs=(
            P(DP, "z"),
            P(DP, "z"),
            P(DP),
            P(DP),
            P(DP),
            P("z", DP, None),
            P("z", DP, None),
            P("z", DP, None),
            P(DP, "z"),
            P("z"),
            P(None, "z"),
        ),
        out_specs=(P("z", DP, None), P(None, "z")),
        check_vma=False,
    )
```

```python
import math

import jax
import jax.numpy as jnp
from jax import lax
from jax.sharding import Mesh
from jax.sharding import PartitionSpec as P

MODEL_WIDTH = 16384
SEQLEN = 128
GROUP = 8
DECODE_STEPS = 4
RANK = 64
BATCH = 16
BLOCK = 2048
TILE = 256
EARLY = 512
OWN = 32

adapter_alpha = 2.0
beta_one = 0.9
beta_two = 0.999
rate = 0.1
adam_count = 200.0
scale = adapter_alpha / (RANK * math.sqrt(MODEL_WIDTH))

bf16 = jnp.bfloat16
f32 = jnp.float32
HIGHEST = lax.Precision.HIGHEST

AXES = ("x", "ya", "yb", "yc", "core", "z")
DP = ("x", "ya", "yb", "yc", "core")
XY = ("x", "ya", "yb", "yc")
MINOR = ("yb", "yc", "core")
CROSS = ("x", "ya", "z")


def swap(chunks, axes):
    return lax.all_to_all(chunks, axes, 0, 0, tiled=False)


def share(piece, axes, count):
    return swap(jnp.broadcast_to(piece[None], (count,) + piece.shape), axes)


def core_swap(value):
    return lax.ppermute(value, "core", [(0, 1), (1, 0)])


def high_low(value):
    high = lax.reduce_precision(value, 8, 7)
    return high.astype(bf16), (value - high).astype(bf16)


def pick(value, index, axis):
    return lax.dynamic_index_in_dim(value, index, axis, keepdims=False)


def body(
    tokens,
    cotangent,
    prompt_len,
    resp_len,
    ranks,
    factors,
    first_moment,
    second_moment,
    base_weight,
    gain,
    state,
):
    core = lax.axis_index("core")
    z = lax.axis_index("z")
    major = lax.axis_index(("x", "ya"))
    minor = lax.axis_index(MINOR)

    left = lax.all_gather(base_weight[:, :EARLY], "z", axis=0, tiled=False)

    positions = jnp.arange(SEQLEN, dtype=jnp.int32)
    lower = prompt_len[:, None]
    upper = lower + resp_len[:, None]
    inside = (positions[None, :] >= lower) & (positions[None, :] < upper)
    advantage = (2 * ranks - (GROUP - 1)).astype(f32) / (GROUP - 1)
    per_seq = advantage / resp_len.astype(f32)
    weight = jnp.where(inside, per_seq[:, None], f32(0.0)).reshape(-1)
    weighted = (cotangent.astype(f32) * weight[:, None]).astype(bf16)
    weighted = lax.optimization_barrier(weighted)

    mine = share(factors[0].astype(bf16), XY, 32)
    other = core_swap(mine)
    low = jnp.where(core == 0, jnp.stack([mine, other], 1), jnp.stack([other, mine], 1))
    low = low.reshape(BLOCK, 2 * RANK)
    hidden = jnp.dot(tokens, low[:, :RANK], preferred_element_type=f32)
    projected = jnp.dot(weighted, low[:, RANK:], preferred_element_type=f32)
    state_tile = lax.dynamic_slice_in_dim(state, minor * TILE, TILE, 1)
    tile_gain = lax.dynamic_slice_in_dim(gain, minor * TILE, TILE, 0)
    sent = jnp.concatenate(
        [
            jnp.concatenate([hidden, projected], axis=1).astype(bf16),
            state_tile.reshape(32, 128),
            *[part.reshape(2, 128) for part in high_low(tile_gain)],
        ],
        axis=0,
    )
    got = share(sent, "z", 8)
    got, later = lax.optimization_barrier((got, base_weight))
    right = lax.all_gather(later[:, EARLY:], "z", axis=0, tiled=False)
    both = jnp.sum(got[:, :SEQLEN].astype(f32), axis=0).astype(bf16)
    home = pick(got[:, SEQLEN:], major, 0)
    first = home[:32].reshape(BATCH, TILE)
    tile_gain = home[32:].astype(f32)
    tile_gain = (tile_gain[:2] + tile_gain[2:]).reshape(TILE)
    own_state = lax.dynamic_slice_in_dim(first, 2 * z, 2, 0)

    dims = (((0,), (0,)), ((), ()))
    grad_down = lax.dot_general(tokens, both[:, RANK:], dims, preferred_element_type=f32)
    grad_up = lax.dot_general(weighted, both[:, :RANK], dims, preferred_element_type=f32)
    grads = jnp.concatenate([grad_down, grad_up], axis=1).astype(bf16).reshape(32, 2, OWN, 128)
    first = jnp.dot(first, base_weight, preferred_element_type=f32)
    first = first.reshape(4, 2, 2, 8, TILE)

    def half(which):
        base = pick(first, which, 1).transpose(2, 0, 1, 3).reshape(32, 4, 128)
        return pick(grads, which, 1), base

    give, give_base = half(1 - core)
    keep, keep_base = half(core)
    got = core_swap(jnp.concatenate([give, *high_low(give_base)], axis=1)).astype(f32)
    keep = (keep.astype(f32) + got[:, :OWN]).astype(bf16)
    keep_base = keep_base + got[:, OWN : OWN + 4] + got[:, OWN + 4 :]
    got = swap(jnp.concatenate([keep, *high_low(keep_base)], axis=1), XY).astype(f32)
    got = jnp.sum(got, axis=0)
    base = got[OWN : OWN + 4] + got[OWN + 4 :]
    own_grads = got[:OWN]
    old = jnp.concatenate([factors[0], first_moment[0], second_moment[0]], axis=0)
    got = lax.ppermute(
        jnp.concatenate([own_grads.astype(bf16), old.astype(bf16), *high_low(base)], axis=0),
        AXES,
        [((k * 8 + i) * 8 + t, (t * 8 + k) * 8 + i) for k in range(8) for i in range(8) for t in range(8)],
    )
    base = (got[4 * OWN : 4 * OWN + 4].astype(f32) + got[4 * OWN + 4 :].astype(f32)).reshape(2, TILE)
    base = base + own_state.astype(f32)
    own_grads = scale * own_grads
    squared = jnp.broadcast_to(jnp.sum(own_grads * own_grads), (1, 128))
    squared = jnp.sum(share(squared, DP, 64), axis=0)
    got = share(jnp.concatenate([got[: 4 * OWN], *high_low(squared)], axis=0), "z", 8).astype(f32)
    grads = scale * got[:, :OWN].reshape(TILE, 128)
    former = got[:, OWN : 4 * OWN]
    squared = jnp.sum(got[:, 4 * OWN :], axis=(0, 1))[None]

    clip = jnp.minimum(f32(1.0), f32(1.0) / (jnp.sqrt(squared) + 1e-06))
    grads = clip * grads

    def update(values, first, second, slopes):
        moment_one = beta_one * first + (1.0 - beta_one) * slopes
        moment_two = beta_two * second + (1.0 - beta_two) * slopes * slopes
        step_size = (
            moment_one
            / (1.0 - beta_one**adam_count)
            / (jnp.sqrt(moment_two / (1.0 - beta_two**adam_count)) + 1e-08)
        )
        return values - rate * step_size

    own_grads = clip * own_grads
    new_factors = update(factors[0], first_moment[0], second_moment[0], own_grads)[None]

    near = update(
        former[:, :OWN].reshape(TILE, 128),
        former[:, OWN : 2 * OWN].reshape(TILE, 128),
        former[:, 2 * OWN :].reshape(TILE, 128),
        grads,
    )
    down = near[:, :RANK].astype(bf16)
    up = near[:, RANK:].astype(bf16).astype(f32).T

    thin = jnp.dot(own_state, down, preferred_element_type=f32).reshape(1, 128)
    thin = jnp.sum(share(thin, DP, 64), axis=0).reshape(2, RANK)
    resid = base + scale * jnp.dot(thin, up, precision=HIGHEST)

    def packed(sums):
        halves = [jnp.broadcast_to(half[:, None], (2, 32)) for half in high_low(sums)]
        return jnp.concatenate(halves, axis=1).reshape(1, 128)

    for step in range(1, DECODE_STEPS):
        own = (resid * tile_gain).astype(bf16)
        thin = jnp.dot(own, down, preferred_element_type=f32).astype(bf16).reshape(1, 128)
        extra = jnp.concatenate([thin, packed(jnp.sum(resid * resid, axis=1))], axis=0)
        value = jnp.broadcast_to(own[None], (8, 2, TILE))
        sums = [
            jnp.einsum("zsk,zkn->zsn", value, panel, preferred_element_type=f32).astype(bf16)
            for panel in (left, right)
        ]
        sums = lax.optimization_barrier(jnp.concatenate(sums, axis=2))
        sums = sums.reshape(8, 2, 8, TILE).transpose(0, 2, 1, 3).reshape(64, 4, 128)
        sent = jnp.concatenate([sums, jnp.broadcast_to(extra[None], (64, 2, 128))], axis=1)
        got = jnp.sum(swap(sent, DP).astype(f32), axis=0)
        thin = got[4].reshape(2, RANK)
        squares = got[5].reshape(2, 2, 32)[:, :, 0]
        norm = lax.rsqrt((squares[:, :1] + squares[:, 1:]) / MODEL_WIDTH + 1e-05)
        total = own.astype(f32) + got[:4].reshape(2, TILE)
        resid = norm * (total + scale * jnp.dot(thin, up, precision=HIGHEST))

    own = (resid * tile_gain).astype(bf16).reshape(4, 128)
    sent = jnp.concatenate([own, packed(jnp.sum(resid * resid, axis=1))], axis=0)
    got = share(sent, CROSS, 64).reshape(8, 8, 5, 128)
    sums = jnp.sum(got[:, :, 4].astype(f32), axis=0).reshape(BATCH, 2, 32)[:, :, :8]
    sums = (sums[:, 0] + sums[:, 1]).reshape(1, 128)
    sent = jnp.concatenate([pick(got[:, :, :4], z, 0).reshape(32, 128), *high_low(sums)], axis=0)
    got = share(sent, MINOR, 8)
    sums = jnp.sum(got[:, 32:].astype(f32), axis=(0, 1)).reshape(BATCH, 8)[:, :1]
    norm = lax.rsqrt(sums / MODEL_WIDTH + 1e-05)
    result = got[:, :32].reshape(8, BATCH, TILE).transpose(1, 0, 2).reshape(BATCH, BLOCK)
    result = (result.astype(f32) * norm).astype(bf16)
    return (new_factors, result)


def solution(mesh):
    fine = Mesh(mesh.devices.reshape(4, 2, 2, 2, 2, 8), AXES)
    return jax.shard_map(
        body,
        mesh=fine,
        in_specs=(
            P(DP, "z"),
            P(DP, "z"),
            P(DP),
            P(DP),
            P(DP),
            P("z", DP, None),
            P("z", DP, None),
            P("z", DP, None),
            P(DP, "z"),
            P("z"),
            P(None, "z"),
        ),
        out_specs=(P("z", DP, None), P(None, "z")),
        check_vma=False,
    )
```

```python
import math

import jax
import jax.numpy as jnp
from jax import lax
from jax.sharding import Mesh
from jax.sharding import PartitionSpec as P

MODEL_WIDTH = 16384
SEQLEN = 128
GROUP = 8
DECODE_STEPS = 4
RANK = 64
BATCH = 16
BLOCK = 2048
TILE = 256
OWN = 32

adapter_alpha = 2.0
beta_one = 0.9
beta_two = 0.999
rate = 0.1
adam_count = 200.0
scale = adapter_alpha / (RANK * math.sqrt(MODEL_WIDTH))

bf16 = jnp.bfloat16
f32 = jnp.float32
HIGHEST = lax.Precision.HIGHEST

AXES = ("x", "ya", "yb", "yc", "core", "z")
DP = ("x", "ya", "yb", "yc", "core")
XY = ("x", "ya", "yb", "yc")
MINOR = ("yb", "yc", "core")
CROSS = ("x", "ya", "z")


def swap(chunks, axes):
    return lax.all_to_all(chunks, axes, 0, 0, tiled=False)


def share(piece, axes, count):
    return swap(jnp.broadcast_to(piece[None], (count,) + piece.shape), axes)


def core_swap(value):
    return lax.ppermute(value, "core", [(0, 1), (1, 0)])


def high_low(value):
    high = lax.reduce_precision(value, 8, 7)
    return high.astype(bf16), (value - high).astype(bf16)


def pick(value, index, axis):
    return lax.dynamic_index_in_dim(value, index, axis, keepdims=False)


def body(
    tokens,
    cotangent,
    prompt_len,
    resp_len,
    ranks,
    factors,
    first_moment,
    second_moment,
    base_weight,
    gain,
    state,
):
    core = lax.axis_index("core")
    z = lax.axis_index("z")
    major = lax.axis_index(("x", "ya"))
    minor = lax.axis_index(MINOR)

    panel = lax.all_gather(base_weight, "z", axis=0, tiled=False)

    positions = jnp.arange(SEQLEN, dtype=jnp.int32)
    lower = prompt_len[:, None]
    upper = lower + resp_len[:, None]
    inside = (positions[None, :] >= lower) & (positions[None, :] < upper)
    advantage = (2 * ranks - (GROUP - 1)).astype(f32) / (GROUP - 1)
    per_seq = advantage / resp_len.astype(f32)
    weight = jnp.where(inside, per_seq[:, None], f32(0.0)).reshape(-1)
    weighted = (cotangent.astype(f32) * weight[:, None]).astype(bf16)
    weighted = lax.optimization_barrier(weighted)

    mine = share(factors[0].astype(bf16), XY, 32)
    other = core_swap(mine)
    low = jnp.where(core == 0, jnp.stack([mine, other], 1), jnp.stack([other, mine], 1))
    low = low.reshape(BLOCK, 2 * RANK)
    hidden = jnp.dot(tokens, low[:, :RANK], preferred_element_type=f32)
    projected = jnp.dot(weighted, low[:, RANK:], preferred_element_type=f32)
    state_tile = lax.dynamic_slice_in_dim(state, minor * TILE, TILE, 1)
    tile_gain = lax.dynamic_slice_in_dim(gain, minor * TILE, TILE, 0)
    sent = jnp.concatenate(
        [
            jnp.concatenate([hidden, projected], axis=1).astype(bf16),
            state_tile.reshape(32, 128),
            *[part.reshape(2, 128) for part in high_low(tile_gain)],
        ],
        axis=0,
    )
    got = share(sent, "z", 8)
    both = jnp.sum(got[:, :SEQLEN].astype(f32), axis=0).astype(bf16)
    home = pick(got[:, SEQLEN:], major, 0)
    first = home[:32].reshape(BATCH, TILE)
    tile_gain = home[32:].astype(f32)
    tile_gain = (tile_gain[:2] + tile_gain[2:]).reshape(TILE)
    own_state = lax.dynamic_slice_in_dim(first, 2 * z, 2, 0)

    dims = (((0,), (0,)), ((), ()))
    grad_down = lax.dot_general(tokens, both[:, RANK:], dims, preferred_element_type=f32)
    grad_up = lax.dot_general(weighted, both[:, :RANK], dims, preferred_element_type=f32)
    grads = jnp.concatenate([grad_down, grad_up], axis=1).astype(bf16).reshape(32, 2, OWN, 128)
    first = jnp.dot(first, base_weight, preferred_element_type=f32)
    first = first.reshape(4, 2, 2, 8, TILE)

    def half(which):
        base = pick(first, which, 1).transpose(2, 0, 1, 3).reshape(32, 4, 128)
        return pick(grads, which, 1), base

    give, give_base = half(1 - core)
    keep, keep_base = half(core)
    got = core_swap(jnp.concatenate([give, *high_low(give_base)], axis=1)).astype(f32)
    keep = (keep.astype(f32) + got[:, :OWN]).astype(bf16)
    keep_base = keep_base + got[:, OWN : OWN + 4] + got[:, OWN + 4 :]
    got = swap(jnp.concatenate([keep, *high_low(keep_base)], axis=1), XY).astype(f32)
    got = jnp.sum(got, axis=0)
    base = got[OWN : OWN + 4] + got[OWN + 4 :]
    own_grads = got[:OWN]
    old = jnp.concatenate([factors[0], first_moment[0], second_moment[0]], axis=0)
    got = lax.ppermute(
        jnp.concatenate([own_grads.astype(bf16), old.astype(bf16), *high_low(base)], axis=0),
        AXES,
        [((k * 8 + i) * 8 + t, (t * 8 + k) * 8 + i) for k in range(8) for i in range(8) for t in range(8)],
    )
    base = (got[4 * OWN : 4 * OWN + 4].astype(f32) + got[4 * OWN + 4 :].astype(f32)).reshape(2, TILE)
    base = base + own_state.astype(f32)
    own_grads = scale * own_grads
    squared = jnp.broadcast_to(jnp.sum(own_grads * own_grads), (1, 128))
    squared = jnp.sum(share(squared, DP, 64), axis=0)
    got = share(jnp.concatenate([got[: 4 * OWN], *high_low(squared)], axis=0), "z", 8).astype(f32)
    grads = scale * got[:, :OWN].reshape(TILE, 128)
    former = got[:, OWN : 4 * OWN]
    squared = jnp.sum(got[:, 4 * OWN :], axis=(0, 1))[None]

    clip = jnp.minimum(f32(1.0), f32(1.0) / (jnp.sqrt(squared) + 1e-06))
    grads = clip * grads

    def update(values, first, second, slopes):
        moment_one = beta_one * first + (1.0 - beta_one) * slopes
        moment_two = beta_two * second + (1.0 - beta_two) * slopes * slopes
        step_size = (
            moment_one
            / (1.0 - beta_one**adam_count)
            / (jnp.sqrt(moment_two / (1.0 - beta_two**adam_count)) + 1e-08)
        )
        return values - rate * step_size

    own_grads = clip * own_grads
    new_factors = update(factors[0], first_moment[0], second_moment[0], own_grads)[None]

    near = update(
        former[:, :OWN].reshape(TILE, 128),
        former[:, OWN : 2 * OWN].reshape(TILE, 128),
        former[:, 2 * OWN :].reshape(TILE, 128),
        grads,
    )
    down = near[:, :RANK].astype(bf16)
    up = near[:, RANK:].astype(bf16).astype(f32).T

    def columns(value, panel):
        value = jnp.broadcast_to(value[None], (8,) + value.shape)
        return jnp.einsum("zsk,zkn->zsn", value, panel, preferred_element_type=f32)

    thin = jnp.dot(own_state, down, preferred_element_type=f32).reshape(1, 128)
    inner = share(thin, DP, 64)
    ahead = columns((jnp.concatenate([up, base], axis=0) * tile_gain).astype(bf16), panel)
    ahead_up = ahead[:, :RANK].astype(bf16)
    inner, ahead_up, ahead = lax.optimization_barrier((inner, ahead_up, ahead[:, RANK:]))
    inner = jnp.sum(inner, axis=0).reshape(2, RANK)
    resid = base + scale * jnp.dot(inner, up, precision=HIGHEST)

    def packed(sums):
        halves = [jnp.broadcast_to(half[:, None], (2, 32)) for half in high_low(sums)]
        return jnp.concatenate(halves, axis=1).reshape(1, 128)

    for step in range(1, DECODE_STEPS):
        own = (resid * tile_gain).astype(bf16)
        thin = jnp.dot(own, down, preferred_element_type=f32).astype(bf16).reshape(1, 128)
        extra = jnp.concatenate([thin, packed(jnp.sum(resid * resid, axis=1))], axis=0)
        if step == 1:
            sums = columns(jnp.concatenate(high_low(inner), axis=0), ahead_up)
            sums = ahead + scale * (sums[:, :2] + sums[:, 2:])
        else:
            sums = columns(own, panel)
        sums = lax.optimization_barrier(sums.astype(bf16))
        sums = sums.reshape(8, 2, 8, TILE).transpose(0, 2, 1, 3).reshape(64, 4, 128)
        sent = jnp.concatenate([sums, jnp.broadcast_to(extra[None], (64, 2, 128))], axis=1)
        got = jnp.sum(swap(sent, DP).astype(f32), axis=0)
        thin = got[4].reshape(2, RANK)
        squares = got[5].reshape(2, 2, 32)[:, :, 0]
        norm = lax.rsqrt((squares[:, :1] + squares[:, 1:]) / MODEL_WIDTH + 1e-05)
        total = own.astype(f32) + got[:4].reshape(2, TILE)
        resid = norm * (total + scale * jnp.dot(thin, up, precision=HIGHEST))

    own = (resid * tile_gain).astype(bf16).reshape(4, 128)
    sent = jnp.concatenate([own, packed(jnp.sum(resid * resid, axis=1))], axis=0)
    got = share(sent, CROSS, 64).reshape(8, 8, 5, 128)
    sums = jnp.sum(got[:, :, 4].astype(f32), axis=0).reshape(BATCH, 2, 32)[:, :, :8]
    sums = (sums[:, 0] + sums[:, 1]).reshape(1, 128)
    sent = jnp.concatenate([pick(got[:, :, :4], z, 0).reshape(32, 128), *high_low(sums)], axis=0)
    got = share(sent, MINOR, 8)
    sums = jnp.sum(got[:, 32:].astype(f32), axis=(0, 1)).reshape(BATCH, 8)[:, :1]
    norm = lax.rsqrt(sums / MODEL_WIDTH + 1e-05)
    result = got[:, :32].reshape(8, BATCH, TILE).transpose(1, 0, 2).reshape(BATCH, BLOCK)
    result = (result.astype(f32) * norm).astype(bf16)
    return (new_factors, result)


def solution(mesh):
    fine = Mesh(mesh.devices.reshape(4, 2, 2, 2, 2, 8), AXES)
    return jax.shard_map(
        body,
        mesh=fine,
        in_specs=(
            P(DP, "z"),
            P(DP, "z"),
            P(DP),
            P(DP),
            P(DP),
            P("z", DP, None),
            P("z", DP, None),
            P("z", DP, None),
            P(DP, "z"),
            P("z"),
            P(None, "z"),
        ),
        out_specs=(P("z", DP, None), P(None, "z")),
        check_vma=False,
    )
```

```python
import math

import jax
import jax.numpy as jnp
from jax import lax
from jax.sharding import Mesh
from jax.sharding import PartitionSpec as P

MODEL_WIDTH = 16384
SEQLEN = 128
GROUP = 8
DECODE_STEPS = 4
RANK = 64
BATCH = 16
BLOCK = 2048
TILE = 256
OWN = 32

adapter_alpha = 2.0
beta_one = 0.9
beta_two = 0.999
rate = 0.1
adam_count = 200.0
scale = adapter_alpha / (RANK * math.sqrt(MODEL_WIDTH))

bf16 = jnp.bfloat16
f32 = jnp.float32
HIGHEST = lax.Precision.HIGHEST

AXES = ("x", "ya", "yb", "yc", "core", "z")
DP = ("x", "ya", "yb", "yc", "core")
XY = ("x", "ya", "yb", "yc")
MINOR = ("yb", "yc", "core")
CROSS = ("x", "ya", "z")


def swap(chunks, axes):
    return lax.all_to_all(chunks, axes, 0, 0, tiled=False)


def share(piece, axes, count):
    return swap(jnp.broadcast_to(piece[None], (count,) + piece.shape), axes)


def core_swap(value):
    return lax.ppermute(value, "core", [(0, 1), (1, 0)])


def high_low(value):
    high = lax.reduce_precision(value, 8, 7)
    return high.astype(bf16), (value - high).astype(bf16)


def pick(value, index, axis):
    return lax.dynamic_index_in_dim(value, index, axis, keepdims=False)


def body(
    tokens,
    cotangent,
    prompt_len,
    resp_len,
    ranks,
    factors,
    first_moment,
    second_moment,
    base_weight,
    gain,
    state,
):
    core = lax.axis_index("core")
    z = lax.axis_index("z")
    major = lax.axis_index(("x", "ya"))
    minor = lax.axis_index(MINOR)

    panel = lax.all_gather(base_weight, "z", axis=0, tiled=False)

    positions = jnp.arange(SEQLEN, dtype=jnp.int32)
    lower = prompt_len[:, None]
    upper = lower + resp_len[:, None]
    inside = (positions[None, :] >= lower) & (positions[None, :] < upper)
    advantage = (2 * ranks - (GROUP - 1)).astype(f32) / (GROUP - 1)
    per_seq = advantage / resp_len.astype(f32)
    weight = jnp.where(inside, per_seq[:, None], f32(0.0)).reshape(-1)
    weighted = (cotangent.astype(f32) * weight[:, None]).astype(bf16)
    weighted = lax.optimization_barrier(weighted)

    mine = share(factors[0].astype(bf16), XY, 32)
    other = core_swap(mine)
    low = jnp.where(core == 0, jnp.stack([mine, other], 1), jnp.stack([other, mine], 1))
    low = low.reshape(BLOCK, 2 * RANK)
    hidden = jnp.dot(tokens, low[:, :RANK], preferred_element_type=f32)
    projected = jnp.dot(weighted, low[:, RANK:], preferred_element_type=f32)
    state_tile = lax.dynamic_slice_in_dim(state, minor * TILE, TILE, 1)
    tile_gain = lax.dynamic_slice_in_dim(gain, minor * TILE, TILE, 0)
    sent = jnp.concatenate(
        [
            jnp.concatenate([hidden, projected], axis=1).astype(bf16),
            state_tile.reshape(32, 128),
            *[part.reshape(2, 128) for part in high_low(tile_gain)],
        ],
        axis=0,
    )
    got = share(sent, "z", 8)
    both = jnp.sum(got[:, :SEQLEN].astype(f32), axis=0).astype(bf16)
    home = pick(got[:, SEQLEN:], major, 0)
    first = home[:32].reshape(BATCH, TILE)
    tile_gain = home[32:].astype(f32)
    tile_gain = (tile_gain[:2] + tile_gain[2:]).reshape(TILE)
    own_state = lax.dynamic_slice_in_dim(first, 2 * z, 2, 0)

    dims = (((0,), (0,)), ((), ()))
    grad_down = lax.dot_general(tokens, both[:, RANK:], dims, preferred_element_type=f32)
    grad_up = lax.dot_general(weighted, both[:, :RANK], dims, preferred_element_type=f32)
    grads = jnp.concatenate([grad_down, grad_up], axis=1).astype(bf16).reshape(32, 2, OWN, 128)
    first = jnp.dot(first, base_weight, preferred_element_type=f32)
    first = first.reshape(4, 2, 2, 8, TILE)

    def half(which):
        base = pick(first, which, 1).transpose(2, 0, 1, 3).reshape(32, 4, 128)
        return pick(grads, which, 1), base

    give, give_base = half(1 - core)
    keep, keep_base = half(core)
    got = core_swap(jnp.concatenate([give, *high_low(give_base)], axis=1)).astype(f32)
    keep = (keep.astype(f32) + got[:, :OWN]).astype(bf16)
    keep_base = keep_base + got[:, OWN : OWN + 4] + got[:, OWN + 4 :]
    got = swap(jnp.concatenate([keep, *high_low(keep_base)], axis=1), XY).astype(f32)
    got = jnp.sum(got, axis=0)
    base = got[OWN : OWN + 4] + got[OWN + 4 :]
    own_grads = got[:OWN]
    old = jnp.concatenate([factors[0], first_moment[0], second_moment[0]], axis=0)
    got = lax.ppermute(
        jnp.concatenate([own_grads.astype(bf16), old.astype(bf16), *high_low(base)], axis=0),
        AXES,
        [((k * 8 + i) * 8 + t, (t * 8 + k) * 8 + i) for k in range(8) for i in range(8) for t in range(8)],
    )
    base = (got[4 * OWN : 4 * OWN + 4].astype(f32) + got[4 * OWN + 4 :].astype(f32)).reshape(2, TILE)
    base = base + own_state.astype(f32)
    own_grads = scale * own_grads
    squared = jnp.broadcast_to(jnp.sum(own_grads * own_grads), (1, 128))
    squared = jnp.sum(share(squared, DP, 64), axis=0)
    got = share(jnp.concatenate([got[: 4 * OWN], *high_low(squared)], axis=0), "z", 8).astype(f32)
    grads = scale * got[:, :OWN].reshape(TILE, 128)
    former = got[:, OWN : 4 * OWN]
    squared = jnp.sum(got[:, 4 * OWN :], axis=(0, 1))[None]

    clip = jnp.minimum(f32(1.0), f32(1.0) / (jnp.sqrt(squared) + 1e-06))
    grads = clip * grads

    def update(values, first, second, slopes):
        moment_one = beta_one * first + (1.0 - beta_one) * slopes
        moment_two = beta_two * second + (1.0 - beta_two) * slopes * slopes
        step_size = (
            moment_one
            / (1.0 - beta_one**adam_count)
            / (jnp.sqrt(moment_two / (1.0 - beta_two**adam_count)) + 1e-08)
        )
        return values - rate * step_size

    own_grads = clip * own_grads
    new_factors = update(factors[0], first_moment[0], second_moment[0], own_grads)[None]

    near = update(
        former[:, :OWN].reshape(TILE, 128),
        former[:, OWN : 2 * OWN].reshape(TILE, 128),
        former[:, 2 * OWN :].reshape(TILE, 128),
        grads,
    )
    down = near[:, :RANK].astype(bf16)
    up = near[:, RANK:].astype(bf16).astype(f32).T

    def columns(value, panel):
        value = jnp.broadcast_to(value[None], (8,) + value.shape)
        return jnp.einsum("zsk,zkn->zsn", value, panel, preferred_element_type=f32)

    thin = jnp.dot(own_state, down, preferred_element_type=f32).reshape(1, 128)
    inner = share(thin, DP, 64)
    ahead = columns((jnp.concatenate([up, base], axis=0) * tile_gain).astype(bf16), panel)
    ahead_up = ahead[:, :RANK].astype(bf16)
    inner, ahead_up, ahead = lax.optimization_barrier((inner, ahead_up, ahead[:, RANK:]))
    inner = jnp.sum(inner, axis=0).reshape(2, RANK)
    resid = base + scale * jnp.dot(inner, up, precision=HIGHEST)

    def packed(sums):
        halves = [jnp.broadcast_to(half[:, None], (2, 32)) for half in high_low(sums)]
        return jnp.concatenate(halves, axis=1).reshape(1, 128)

    for step in range(1, DECODE_STEPS):
        own = (resid * tile_gain).astype(bf16)
        thin = jnp.dot(own, down, preferred_element_type=f32).astype(bf16).reshape(1, 128)
        extra = jnp.concatenate([thin, packed(jnp.sum(resid * resid, axis=1))], axis=0)
        if step == 1:
            sums = columns(jnp.concatenate(high_low(inner), axis=0), ahead_up)
            sums = ahead + scale * (sums[:, :2] + sums[:, 2:])
        else:
            sums = columns(own, panel)
        sums = lax.optimization_barrier(sums.astype(bf16))
        sums = sums.reshape(8, 2, 8, TILE).transpose(0, 2, 1, 3).reshape(64, 4, 128)
        sent = jnp.concatenate([sums, jnp.broadcast_to(extra[None], (64, 2, 128))], axis=1)
        got = jnp.sum(swap(sent, DP).astype(f32), axis=0)
        thin = got[4].reshape(2, RANK)
        squares = got[5].reshape(2, 2, 32)[:, :, 0]
        norm = lax.rsqrt((squares[:, :1] + squares[:, 1:]) / MODEL_WIDTH + 1e-05)
        total = own.astype(f32) + got[:4].reshape(2, TILE)
        resid = norm * (total + scale * jnp.dot(thin, up, precision=HIGHEST))

    own = (resid * tile_gain).astype(bf16).reshape(4, 128)
    sent = jnp.concatenate([own, packed(jnp.sum(resid * resid, axis=1))], axis=0)
    got = share(sent, DP, 64)
    sums = jnp.sum(got[:, 4].astype(f32), axis=0).reshape(2, 2, 32)[:, :, 0]
    norm = lax.rsqrt((sums[:, :1] + sums[:, 1:]) / MODEL_WIDTH + 1e-05)
    result = got[:, :4].reshape(8, 8, 2, TILE).transpose(0, 2, 1, 3).reshape(8, 2, BLOCK)
    result = (result.astype(f32) * norm).astype(bf16)
    result = swap(result, "z").reshape(BATCH, BLOCK)
    return (new_factors, result)


def solution(mesh):
    fine = Mesh(mesh.devices.reshape(4, 2, 2, 2, 2, 8), AXES)
    return jax.shard_map(
        body,
        mesh=fine,
        in_specs=(
            P(DP, "z"),
            P(DP, "z"),
            P(DP),
            P(DP),
            P(DP),
            P("z", DP, None),
            P("z", DP, None),
            P("z", DP, None),
            P(DP, "z"),
            P("z"),
            P(None, "z"),
        ),
        out_specs=(P("z", DP, None), P(None, "z")),
        check_vma=False,
    )
```

```python
import math

import jax
import jax.numpy as jnp
from jax import lax
from jax.sharding import Mesh
from jax.sharding import PartitionSpec as P

MODEL_WIDTH = 16384
SEQLEN = 128
GROUP = 8
DECODE_STEPS = 4
RANK = 64
BATCH = 16
BLOCK = 2048
TILE = 256
OWN = 32

adapter_alpha = 2.0
beta_one = 0.9
beta_two = 0.999
rate = 0.1
adam_count = 200.0
scale = adapter_alpha / (RANK * math.sqrt(MODEL_WIDTH))

bf16 = jnp.bfloat16
f32 = jnp.float32
HIGHEST = lax.Precision.HIGHEST

AXES = ("x", "ya", "yb", "yc", "core", "z")
DP = ("x", "ya", "yb", "yc", "core")
XY = ("x", "ya", "yb", "yc")
MINOR = ("yb", "yc", "core")
CROSS = ("x", "ya", "z")


def swap(chunks, axes):
    return lax.all_to_all(chunks, axes, 0, 0, tiled=False)


def share(piece, axes, count):
    return swap(jnp.broadcast_to(piece[None], (count,) + piece.shape), axes)


def core_swap(value):
    return lax.ppermute(value, "core", [(0, 1), (1, 0)])


def high_low(value):
    high = lax.reduce_precision(value, 8, 7)
    return high.astype(bf16), (value - high).astype(bf16)


def pick(value, index, axis):
    return lax.dynamic_index_in_dim(value, index, axis, keepdims=False)


def body(
    tokens,
    cotangent,
    prompt_len,
    resp_len,
    ranks,
    factors,
    first_moment,
    second_moment,
    base_weight,
    gain,
    state,
):
    core = lax.axis_index("core")
    z = lax.axis_index("z")
    major = lax.axis_index(("x", "ya"))
    minor = lax.axis_index(MINOR)

    panel = lax.all_gather(base_weight, "z", axis=0, tiled=False)

    positions = jnp.arange(SEQLEN, dtype=jnp.int32)
    lower = prompt_len[:, None]
    upper = lower + resp_len[:, None]
    inside = (positions[None, :] >= lower) & (positions[None, :] < upper)
    advantage = (2 * ranks - (GROUP - 1)).astype(f32) / (GROUP - 1)
    per_seq = advantage / resp_len.astype(f32)
    weight = jnp.where(inside, per_seq[:, None], f32(0.0)).reshape(-1)
    weighted = (cotangent.astype(f32) * weight[:, None]).astype(bf16)
    weighted = lax.optimization_barrier(weighted)

    mine = share(factors[0].astype(bf16), XY, 32)
    other = core_swap(mine)
    low = jnp.where(core == 0, jnp.stack([mine, other], 1), jnp.stack([other, mine], 1))
    low = low.reshape(BLOCK, 2 * RANK)
    hidden = jnp.dot(tokens, low[:, :RANK], preferred_element_type=f32)
    projected = jnp.dot(weighted, low[:, RANK:], preferred_element_type=f32)
    state_tile = lax.dynamic_slice_in_dim(state, minor * TILE, TILE, 1)
    tile_gain = lax.dynamic_slice_in_dim(gain, minor * TILE, TILE, 0)
    sent = jnp.concatenate(
        [
            jnp.concatenate([hidden, projected], axis=1).astype(bf16),
            state_tile.reshape(32, 128),
            *[part.reshape(2, 128) for part in high_low(tile_gain)],
        ],
        axis=0,
    )
    got = share(sent, "z", 8)
    both = jnp.sum(got[:, :SEQLEN].astype(f32), axis=0).astype(bf16)
    home = pick(got[:, SEQLEN:], major, 0)
    first = home[:32].reshape(BATCH, TILE)
    tile_gain = home[32:].astype(f32)
    tile_gain = (tile_gain[:2] + tile_gain[2:]).reshape(TILE)
    own_state = lax.dynamic_slice_in_dim(first, 2 * z, 2, 0)

    dims = (((0,), (0,)), ((), ()))
    grad_down = lax.dot_general(tokens, both[:, RANK:], dims, preferred_element_type=f32)
    grad_up = lax.dot_general(weighted, both[:, :RANK], dims, preferred_element_type=f32)
    grads = jnp.concatenate([grad_down, grad_up], axis=1).astype(bf16).reshape(32, 2, OWN, 128)
    first = jnp.dot(first, base_weight, preferred_element_type=f32)
    first = first.reshape(4, 2, 2, 8, TILE)

    def half(which):
        base = pick(first, which, 1).transpose(2, 0, 1, 3).reshape(32, 4, 128)
        return pick(grads, which, 1), base

    give, give_base = half(1 - core)
    keep, keep_base = half(core)
    got = core_swap(jnp.concatenate([give, *high_low(give_base)], axis=1)).astype(f32)
    keep = (keep.astype(f32) + got[:, :OWN]).astype(bf16)
    keep_base = keep_base + got[:, OWN : OWN + 4] + got[:, OWN + 4 :]
    got = swap(jnp.concatenate([keep, *high_low(keep_base)], axis=1), XY).astype(f32)
    got = jnp.sum(got, axis=0)
    base = got[OWN : OWN + 4] + got[OWN + 4 :]
    own_grads = got[:OWN]
    old = jnp.concatenate([factors[0], first_moment[0], second_moment[0]], axis=0)
    got = lax.ppermute(
        jnp.concatenate([own_grads.astype(bf16), old.astype(bf16), *high_low(base)], axis=0),
        AXES,
        [((k * 8 + i) * 8 + t, (t * 8 + k) * 8 + i) for k in range(8) for i in range(8) for t in range(8)],
    )
    base = (got[4 * OWN : 4 * OWN + 4].astype(f32) + got[4 * OWN + 4 :].astype(f32)).reshape(2, TILE)
    base = base + own_state.astype(f32)
    own_grads = scale * own_grads
    squared = jnp.sum(own_grads * own_grads, axis=0, keepdims=True)
    squared = jnp.sum(share(squared, DP, 64), axis=0)
    got = share(jnp.concatenate([got[: 4 * OWN], *high_low(squared)], axis=0), "z", 8).astype(f32)
    grads = scale * got[:, :OWN].reshape(TILE, 128)
    former = got[:, OWN : 4 * OWN]
    squared = jnp.sum(got[:, 4 * OWN :])

    clip = jnp.minimum(f32(1.0), f32(1.0) / (jnp.sqrt(squared) + 1e-06))
    grads = clip * grads

    def update(values, first, second, slopes):
        moment_one = beta_one * first + (1.0 - beta_one) * slopes
        moment_two = beta_two * second + (1.0 - beta_two) * slopes * slopes
        step_size = (
            moment_one
            / (1.0 - beta_one**adam_count)
            / (jnp.sqrt(moment_two / (1.0 - beta_two**adam_count)) + 1e-08)
        )
        return values - rate * step_size

    own_grads = clip * own_grads
    new_factors = update(factors[0], first_moment[0], second_moment[0], own_grads)[None]

    near = update(
        former[:, :OWN].reshape(TILE, 128),
        former[:, OWN : 2 * OWN].reshape(TILE, 128),
        former[:, 2 * OWN :].reshape(TILE, 128),
        grads,
    )
    down = near[:, :RANK].astype(bf16)
    up = near[:, RANK:].astype(bf16).astype(f32).T

    def columns(value, panel):
        value = jnp.broadcast_to(value[None], (8,) + value.shape)
        return jnp.einsum("zsk,zkn->zsn", value, panel, preferred_element_type=f32)

    thin = jnp.dot(own_state, down, preferred_element_type=f32).reshape(1, 128)
    inner = share(thin, DP, 64)
    ahead = columns((jnp.concatenate([up, base], axis=0) * tile_gain).astype(bf16), panel)
    ahead_up = ahead[:, :RANK].astype(bf16)
    inner, ahead_up, ahead = lax.optimization_barrier((inner, ahead_up, ahead[:, RANK:]))
    inner = jnp.sum(inner, axis=0).reshape(2, RANK)
    resid = base + scale * jnp.dot(inner, up, precision=HIGHEST)

    def packed(sums):
        halves = [jnp.broadcast_to(half[:, None], (2, 32)) for half in high_low(sums)]
        return jnp.concatenate(halves, axis=1).reshape(1, 128)

    for step in range(1, DECODE_STEPS):
        own = (resid * tile_gain).astype(bf16)
        thin = jnp.dot(own, down, preferred_element_type=f32).astype(bf16).reshape(1, 128)
        extra = jnp.concatenate([thin, packed(jnp.sum(resid * resid, axis=1))], axis=0)
        if step == 1:
            sums = columns(jnp.concatenate(high_low(inner), axis=0), ahead_up)
            sums = ahead + scale * (sums[:, :2] + sums[:, 2:])
        else:
            sums = columns(own, panel)
        sums = lax.optimization_barrier(sums.astype(bf16))
        sums = sums.reshape(8, 2, 8, TILE).transpose(0, 2, 1, 3).reshape(64, 4, 128)
        sent = jnp.concatenate([sums, jnp.broadcast_to(extra[None], (64, 2, 128))], axis=1)
        got = jnp.sum(swap(sent, DP).astype(f32), axis=0)
        thin = got[4].reshape(2, RANK)
        squares = got[5].reshape(2, 2, 32)[:, :, 0]
        norm = lax.rsqrt((squares[:, :1] + squares[:, 1:]) / MODEL_WIDTH + 1e-05)
        total = own.astype(f32) + got[:4].reshape(2, TILE)
        resid = norm * (total + scale * jnp.dot(thin, up, precision=HIGHEST))

    own = (resid * tile_gain).astype(bf16).reshape(4, 128)
    sent = jnp.concatenate([own, packed(jnp.sum(resid * resid, axis=1))], axis=0)
    got = share(sent, DP, 64)
    sums = jnp.sum(got[:, 4].astype(f32), axis=0).reshape(2, 2, 32)[:, :, 0]
    norm = lax.rsqrt((sums[:, :1] + sums[:, 1:]) / MODEL_WIDTH + 1e-05)
    result = got[:, :4].reshape(8, 8, 2, TILE).transpose(0, 2, 1, 3).reshape(8, 2, BLOCK)
    result = (result.astype(f32) * norm).astype(bf16)
    result = swap(result, "z").reshape(BATCH, BLOCK)
    return (new_factors, result)


def solution(mesh):
    fine = Mesh(mesh.devices.reshape(4, 2, 2, 2, 2, 8), AXES)
    return jax.shard_map(
        body,
        mesh=fine,
        in_specs=(
            P(DP, "z"),
            P(DP, "z"),
            P(DP),
            P(DP),
            P(DP),
            P("z", DP, None),
            P("z", DP, None),
            P("z", DP, None),
            P(DP, "z"),
            P("z"),
            P(None, "z"),
        ),
        out_specs=(P("z", DP, None), P(None, "z")),
        check_vma=False,
    )
```
